32 devices in a mesh: groups: 2 (over y), tm: 4 (over z), dp: 4 (over x, core).
Axes of the slice: x: 2, y: 2, z: 4, core: 2. Of those that a mesh axis runs over, the one named last changes fastest.
Arguments:
- clips: bfloat16 [8, 8, 8, 32, 384], P(('groups', 'dp'), 'tm'), parts along dimension 0, may hold values from -16 to 16
- cotangent: bfloat16 [8, 8, 8, 32, 384], P(('groups', 'dp'), 'tm'), parts along dimension 0, may hold values from -6 to 6
- spatial_kernel: float32 [7, 7, 384], replicated, may hold values from -0.875 to 0.875
- temporal_kernel: float32 [31, 384], replicated, may hold values from -1 to 1
- norm_gain: float32 [384], replicated, may hold values from 0.1 to 1.9
- w_expand: bfloat16 [384, 1536], replicated, may hold values from -0.3125 to 0.3125
- w_project: bfloat16 [1536, 384], replicated, may hold values from -0.15625 to 0.15625
Outputs:
- block_out: bfloat16 [8, 8, 8, 32, 384], P(('groups', 'dp'), 'tm'), parts along dimension 0
- grad_clips: bfloat16 [8, 8, 8, 32, 384], P(('groups', 'dp'), 'tm'), parts along dimension 0
- grad_expand: float32 [3072, 384], P(('groups', 'tm', 'dp')), parts along dimension 0
The draws below stay inside these ranges and needn't reach their ends.
There are 2 independent parts, one for each index of `groups`. The reference program is written for one: setup_inputs(seed, part) draws one part's arguments, and reference() takes and returns one part's arrays. A program takes and returns all parts, laid end to end along the dimension named above; an argument that names none is the same for every part. Nothing has to cross between parts.
All inputs are finite; a program needn't handle non-finite values.
Results may differ from the reference program's by a relative error of at most 0.0077.
Values may be sent and summed in bfloat16 or wider, within the bound.
No kernel may reach another device: no remote copies, remote signals or barrier semaphores. Data moves between devices by JAX's collectives and lax.ppermute only.
A program may use at most 64 MiB of HBM per device.

```python
import math
import jax
import jax.numpy as jnp
from jax import lax

C = 384
HID = 1536
KS = 7
TAPS = 31
H = 8
W = 32
CLIPS = 4
FRAMES = 8


def draw_clips(key, part):
    key_base = jax.random.fold_in(key, 11)
    key_chan = jax.random.fold_in(key, 12)
    key_cell = jax.random.fold_in(key, 13)
    shape = (CLIPS, FRAMES, H, W, C)
    channel_scale = jnp.exp(jax.random.uniform(key_chan, (C,), jnp.float32, math.log(0.3), math.log(3.0)))
    cell_scale = jnp.exp(jax.random.uniform(key_cell, (CLIPS, FRAMES, H, W, 1), jnp.float32, math.log(0.4), math.log(4.0)))
    base = jax.random.normal(key_base, shape, jnp.float32)
    return jnp.clip(base * channel_scale * cell_scale, -16.0, 16.0).astype(jnp.bfloat16)


def level_of(stream_key, shape, split, least, top_value):
    loudness, own = 1.0, jax.random.fold_in(stream_key, 6)
    for position, shards_of in split:
        heights = jnp.exp(jax.random.uniform(jax.random.fold_in(own, position), (shards_of,), jnp.float32, least / len(split), top_value / len(split)))
        loudness = loudness * jnp.repeat(heights, shape[position] // shards_of).reshape([-1 if axis == position else 1 for axis in range(len(shape))])
    return loudness


def scatter_about(key, shape, spread, reach, pieces=(), dtype=jnp.bfloat16):
    values = spread * jax.random.normal(key, shape, jnp.float32)
    if pieces:
        values = values * level_of(key, shape, pieces, -0.22, 0.18)
    return jnp.clip(values, -reach, reach).astype(dtype)


def setup_inputs(seed: int = 0, part: int = 0) -> dict:
    keys = jax.random.split(jax.random.key(seed), 8)
    part_splits = jax.random.split(jax.random.fold_in(keys[7], part), 8)
    clips = draw_clips(jax.random.fold_in(jax.random.fold_in(keys[7], part), 71), part)
    cotangent = scatter_about(part_splits[1], (CLIPS, FRAMES, H, W, C), 1.0, 6.0, ((0, 4), (1, 4)))
    spatial_kernel = scatter_about(keys[2], (KS, KS, C), (KS * KS) ** -0.5, 0.875, (), jnp.float32)
    temporal_kernel = scatter_about(keys[3], (TAPS, C), TAPS ** -0.5, 1.0, (), jnp.float32)
    norm_gain = jnp.clip(1.0 + 0.18 * jax.random.normal(keys[4], (C,), jnp.float32), 0.1, 1.9)
    w_expand = scatter_about(keys[5], (C, HID), C ** -0.5, 0.3125)
    w_project = scatter_about(keys[6], (HID, C), HID ** -0.5, 0.15625)
    return {"clips": clips, "cotangent": cotangent, "spatial_kernel": spatial_kernel, "temporal_kernel": temporal_kernel, "norm_gain": norm_gain, "w_expand": w_expand, "w_project": w_project}


def spatial_pass(values, kernel, flip):
    radius = kernel.shape[0] // 2
    height = values.shape[-3]
    width = values.shape[-2]
    row_axis = values.ndim - 3
    col_axis = values.ndim - 2
    pads = [(0, 0)] * (values.ndim - 3) + [(radius, radius), (radius, radius), (0, 0)]
    padded = jnp.pad(values, pads)
    summed = jnp.zeros(values.shape, jnp.float32)
    for row_off in range(kernel.shape[0]):
        for col_off in range(kernel.shape[1]):
            first_row = 2 * radius - row_off if flip else row_off
            first_col = 2 * radius - col_off if flip else col_off
            window = lax.slice_in_dim(padded, first_row, first_row + height, axis=row_axis)
            window = lax.slice_in_dim(window, first_col, first_col + width, axis=col_axis)
            summed = summed + kernel[row_off, col_off] * window
    return summed

def time_pass(values, kernel, time_axis, flip):
    radius = kernel.shape[0] // 2
    length = values.shape[time_axis]
    pads = [(0, 0)] * values.ndim
    pads[time_axis] = (radius, radius)
    padded = jnp.pad(values, pads)
    summed = jnp.zeros(values.shape, jnp.float32)
    for lag_index in range(kernel.shape[0]):
        first_pos = 2 * radius - lag_index if flip else lag_index
        summed = summed + kernel[lag_index] * lax.slice_in_dim(padded, first_pos, first_pos + length, axis=time_axis)
    return summed

def gelu_value(preact):
    return 0.5 * preact * (1.0 + lax.erf(preact * 0.7071067811865476))

def gelu_slope(preact):
    return 0.5 * (1.0 + lax.erf(preact * 0.7071067811865476)) + preact * jnp.exp(-0.5 * preact * preact) * 0.3989422804014327

def token_block(tokens, grads, norm_gain, w_expand, w_project):
    values = tokens.astype(jnp.float32)
    average = lax.optimization_barrier(jnp.mean(values, axis=-1, keepdims=True))
    centred = values - average
    inv_std = lax.rsqrt(lax.optimization_barrier(jnp.mean(centred * centred, axis=-1, keepdims=True)) + 1e-06)
    normed = centred * inv_std
    scaled = (normed * norm_gain).astype(jnp.bfloat16)
    preact = jnp.dot(scaled, w_expand, preferred_element_type=jnp.float32)
    hidden = gelu_value(preact).astype(jnp.bfloat16)
    branch = jnp.dot(hidden, w_project, preferred_element_type=jnp.float32).astype(jnp.bfloat16)
    d_hidden = jnp.dot(grads, w_project.T, preferred_element_type=jnp.float32)
    d_pre = (d_hidden * gelu_slope(preact)).astype(jnp.bfloat16)
    d_scaled = jnp.dot(d_pre, w_expand.T, preferred_element_type=jnp.float32)
    d_normed = d_scaled * norm_gain
    d_tokens = inv_std * (d_normed - lax.optimization_barrier(jnp.mean(d_normed, axis=-1, keepdims=True)) - normed * lax.optimization_barrier(jnp.mean(d_normed * normed, axis=-1, keepdims=True)))
    return (branch, d_pre, scaled, d_tokens.astype(jnp.bfloat16))

def reference(clips, cotangent, spatial_kernel, temporal_kernel, norm_gain, w_expand, w_project):

    def one_clip(summed, pair):
        frames_in, grads_in = pair
        first = spatial_pass(frames_in.astype(jnp.float32), spatial_kernel, False).astype(jnp.bfloat16)
        second = time_pass(first.astype(jnp.float32), temporal_kernel, 0, False).astype(jnp.bfloat16)
        branch, d_pre, scaled, d_tokens = token_block(second.reshape(-1, C), grads_in.reshape(-1, C), norm_gain, w_expand, w_project)
        contrib = jnp.dot(d_pre.T, scaled, preferred_element_type=jnp.float32)
        block_out = (frames_in.astype(jnp.float32) + branch.reshape(frames_in.shape).astype(jnp.float32)).astype(jnp.bfloat16)
        d_first = time_pass(d_tokens.reshape(frames_in.shape).astype(jnp.float32), temporal_kernel, 0, True).astype(jnp.bfloat16)
        grad_in = (grads_in.astype(jnp.float32) + spatial_pass(d_first.astype(jnp.float32), spatial_kernel, True)).astype(jnp.bfloat16)
        return (summed + contrib, (block_out, grad_in))
    summed, outputs = lax.scan(one_clip, jnp.zeros((HID, C), jnp.float32), (clips, cotangent))
    scale_factor = float(CLIPS * FRAMES * H * W) ** (-0.5)
    return (outputs[0], outputs[1], summed * scale_factor)
```

```python
import functools
import jax
import jax.numpy as jnp
from jax import lax
from jax.experimental import pallas as pl
from jax.experimental.pallas import tpu as pltpu
from jax.sharding import PartitionSpec as P

LANES = 128
PAD = 8
F32 = jnp.float32
BF16 = jnp.bfloat16
VMEM_LIMIT = 32 * 1024 * 1024


def call(body, outs, scratch, *args, flops=0, limit=VMEM_LIMIT):
    moved = sum(a.size * a.dtype.itemsize for a in args)
    moved += sum(o.size * o.dtype.itemsize for o in outs)
    return pl.pallas_call(
        body,
        out_shape=tuple(outs),
        in_specs=[pl.BlockSpec(memory_space=pltpu.VMEM)] * len(args),
        out_specs=tuple([pl.BlockSpec(memory_space=pltpu.VMEM)] * len(outs)),
        scratch_shapes=list(scratch),
        cost_estimate=pl.CostEstimate(flops=flops, bytes_accessed=moved, transcendentals=0),
        compiler_params=pltpu.CompilerParams(vmem_limit_bytes=limit),
    )(*args)


def struct(shape, dtype):
    return jax.ShapeDtypeStruct(tuple(shape), dtype)


def slot_to(step, count):
    if count == 1:
        return 0
    return lax.rem(lax.axis_index("tm") + step, count)


def slot_from(step, count):
    if count == 1:
        return 0
    return lax.rem(lax.axis_index("tm") + count - step, count)


def exchange(pieces):
    count = len(pieces)
    got = [pieces[0]]
    for step in range(1, count):
        pairs = [(i, (i + step) % count) for i in range(count)]
        got.append(lax.ppermute(pieces[step], "tm", pairs))
    return got


def conv_rows(pad_ref, kernel_ref, block, col, height, flip, emit):
    taps = kernel_ref.shape[1]
    radius = taps // 2
    acc = [None] * height
    for col_off in range(taps):
        shift = radius - col_off if flip else col_off - radius
        weights = [
            kernel_ref[block, row_off, pl.ds(col_off, 1), :] for row_off in range(taps)
        ]
        for row in range(height):
            values = pad_ref[block, :, row, pl.ds(PAD + col + shift, 8), :]
            for row_off in range(taps):
                out = row - radius + row_off if flip else row + radius - row_off
                if 0 <= out < height:
                    term = values * weights[row_off][None]
                    acc[out] = term if acc[out] is None else acc[out] + term
    for row in range(height):
        emit(row, acc[row])


def clear_pads(pad_ref, width):
    blocks, frames, height, _, lanes = pad_ref.shape
    zero = jnp.zeros((blocks, frames, height, PAD, lanes), F32)
    pad_ref[:, :, :, 0:PAD, :] = zero
    pad_ref[:, :, :, PAD + width : PAD + width + PAD, :] = zero


def spatial_fwd(count, *refs):
    clips, cot, kernel = refs[:3]
    firsts = refs[3 : 3 + count]
    cots = refs[3 + count : 3 + 2 * count]
    pad_ref, flat = refs[3 + 2 * count :]
    _, frames, height, width, channels = clips.shape
    blocks = channels // LANES
    pixels = height * width // count
    clear_pads(pad_ref, width)
    for block in range(blocks):
        lanes = slice(block * LANES, (block + 1) * LANES)
        pad_ref[block, :, :, PAD : PAD + width, :] = clips[0, :, :, :, lanes].astype(F32)

    for block in range(blocks):
        lanes = slice(block * LANES, (block + 1) * LANES)
        for col in range(0, width, 8):

            def emit(row, value):
                flat[:, row, pl.ds(col, 8), lanes] = value

            conv_rows(pad_ref, kernel, block, col, height, False, emit)
    rows = height // count
    for step in range(count):
        base = slot_to(step, count) * rows
        firsts[step][...] = (
            flat[:, pl.ds(base, rows), :, :].reshape(frames, pixels, channels).astype(BF16)
        )
        cots[step][...] = cot[0, :, pl.ds(base, rows), :, :].reshape(frames, pixels, channels)


def spatial_bwd(count, *refs):
    pieces = refs[:count]
    cot, kernel, out_ref, pad_ref = refs[count:]
    _, frames, height, width, channels = cot.shape
    blocks = channels // LANES
    rows = height // count
    clear_pads(pad_ref, width)
    for step in range(count):
        base = slot_from(step, count) * rows
        for block in range(blocks):
            lanes = slice(block * LANES, (block + 1) * LANES)
            piece = pieces[step][:, :, lanes].astype(F32).reshape(frames, rows, width, LANES)
            pad_ref[block, :, pl.ds(base, rows), PAD : PAD + width, :] = piece
    for block in range(blocks):
        lanes = slice(block * LANES, (block + 1) * LANES)
        for col in range(0, width, 16):
            halves = []
            for part in range(2):
                rows_out = []
                conv_rows(
                    pad_ref, kernel, block, col + 8 * part, height, True,
                    lambda row, value: rows_out.append(value),
                )
                halves.append(rows_out)
            for row in range(height):
                total = jnp.concatenate([halves[0][row], halves[1][row]], axis=1)
                total = total + cot[0, :, row, pl.ds(col, 16), lanes].astype(F32)
                out_ref[0, :, row, pl.ds(col, 16), lanes] = total.astype(BF16)


def mix_frames(source, target, kernel, flip):
    frames = source.shape[0]
    taps = kernel.shape[0]
    radius = taps // 2
    if frames <= 16:
        for out in range(frames):
            total = None
            for inp in range(frames):
                lag = (out - inp if flip else inp - out) + radius
                if 0 <= lag < taps:
                    term = kernel[pl.ds(lag, 1), :] * source[inp]
                    total = term if total is None else total + term
            target[out] = total.astype(BF16).astype(F32)
        return

    def one(out, carry):
        def tap(inp, total):
            lag = (out - inp if flip else inp - out) + radius
            return total + kernel[pl.ds(lag, 1), :] * source[inp]

        low = jnp.maximum(out - radius, 0)
        high = jnp.minimum(out + radius + 1, frames)
        total = lax.fori_loop(low, high, tap, jnp.zeros(source.shape[1:], F32))
        target[out] = total.astype(BF16).astype(F32)
        return carry

    lax.fori_loop(0, frames, one, 0)


def place_frames(count, pieces, target):
    for step in range(count):
        frames = pieces[step].shape[0]
        base = slot_from(step, count) * frames
        target[pl.ds(base, frames)] = pieces[step][...].astype(target.dtype)


def mlp_fwd(count, chunk, *refs):
    pieces = refs[:count]
    taps, gain, w_expand, w_project = refs[count : count + 4]
    branches = refs[count + 4 : 2 * count + 4]
    scaled, slope, normed, inv_std, mixed_in, mixed, hidden, branch = refs[2 * count + 4 :]
    frames, pixels, channels = mixed_in.shape
    tokens = frames * pixels
    place_frames(count, pieces, mixed_in)
    mix_frames(mixed_in, mixed, taps, False)
    values = mixed[...].reshape(tokens, channels)
    average = jnp.mean(values, axis=-1, keepdims=True)
    centred = values - average
    inverse = lax.rsqrt(jnp.mean(centred * centred, axis=-1, keepdims=True) + 1e-06)
    inv_std[...] = inverse
    norm = centred * inverse
    normed[...] = norm
    scaled[...] = (norm * gain[...]).astype(BF16)
    for start in range(0, w_expand.shape[1], chunk):
        part = slice(start, start + chunk)
        pre = jnp.dot(scaled[...], w_expand[:, part], preferred_element_type=F32)
        cdf = 0.5 + 0.5 * lax.erf(pre * 0.7071067811865476)
        hidden[:, part] = (pre * cdf).astype(BF16)
        slope[:, part] = (cdf + pre * jnp.exp(-0.5 * pre * pre) * 0.3989422804014327).astype(BF16)
    branch[...] = jnp.dot(hidden[...], w_project[...], preferred_element_type=F32).reshape(
        frames, pixels, channels
    )
    own = frames // count
    for step in range(count):
        base = slot_to(step, count) * own
        branches[step][...] = branch[pl.ds(base, own)].astype(BF16)


def mlp_bwd(count, chunk, *refs):
    pieces = refs[:count]
    slope, normed, inv_std, taps, gain, w_expand, w_project = refs[count : count + 7]
    outs = refs[count + 7 : 2 * count + 7]
    d_pre, grads, d_second, d_first = refs[2 * count + 7 :]
    frames, pixels, channels = grads.shape
    tokens = frames * pixels
    place_frames(count, pieces, grads)
    grad_rows = grads[...].reshape(tokens, channels).astype(BF16)
    last = (((1,), (1,)), ((), ()))
    for start in range(0, w_expand.shape[1], chunk):
        part = slice(start, start + chunk)
        d_hidden = lax.dot_general(grad_rows, w_project[part, :], last, preferred_element_type=F32)
        d_pre[:, part] = (d_hidden * slope[:, part].astype(F32)).astype(BF16)
    d_scaled = lax.dot_general(d_pre[...], w_expand[...], last, preferred_element_type=F32)
    d_normed = d_scaled * gain[...]
    norm = normed[...]
    d_tokens = inv_std[...] * (
        d_normed
        - jnp.mean(d_normed, axis=-1, keepdims=True)
        - norm * jnp.mean(d_normed * norm, axis=-1, keepdims=True)
    )
    d_second[...] = d_tokens.astype(BF16).astype(F32).reshape(frames, pixels, channels)
    mix_frames(d_second, d_first, taps, True)
    own = frames // count
    for step in range(count):
        base = slot_to(step, count) * own
        outs[step][...] = d_first[pl.ds(base, own)].astype(BF16)


def add_residual(count, *refs):
    pieces = refs[:count]
    clips, out_ref = refs[count:]
    _, frames, height, width, channels = clips.shape
    rows = height // count
    for step in range(count):
        base = slot_from(step, count) * rows
        piece = pieces[step][...].reshape(frames, rows, width, channels).astype(F32)
        here = (0, slice(None), pl.ds(base, rows))
        out_ref[here] = (clips[here].astype(F32) + piece).astype(BF16)


def weight_grad(d_pre, scaled, keep, send, full):
    block = keep.shape[1]
    full[...] = lax.dot_general(
        d_pre[...], scaled[...], (((0,), (0,)), ((), ())), preferred_element_type=F32
    ).reshape(full.shape)
    core = lax.rem(lax.axis_index("dp"), 2)
    for pair in range(full.shape[0] // 2):
        keep[pair] = full[2 * pair + core]
        send[pair] = full[2 * pair + 1 - core].astype(BF16)


def fold_pair(keep_in, got, keep, send):
    side = lax.div(lax.axis_index("dp"), 2)
    for slot in range(keep.shape[0]):
        mine, other = 2 * slot + side, 2 * slot + 1 - side
        keep[slot] = keep_in[mine] + got[mine].astype(F32)
        send[slot] = (keep_in[other] + got[other].astype(F32)).astype(BF16)


def fold_tm(count, keep_in, got, keep, *sends):
    for step in range(count):
        slot = slot_to(step, count)
        total = keep_in[slot] + got[slot].astype(F32)
        if step == 0:
            keep[...] = total
        else:
            sends[step - 1][...] = total.astype(BF16)


def fold_last(scale_factor, keep_in, *refs):
    total = keep_in[...]
    for got in refs[:-1]:
        total = total + got[...].astype(F32)
    refs[-1][...] = total * scale_factor


def scatter_grad(d_pre, scaled, count, scale_factor):
    hid, channels = d_pre.shape[1], scaled.shape[1]
    sides = lax.axis_size("dp")
    if count == 1 or sides != 4:
        whole = lax.dot_general(
            d_pre, scaled, (((0,), (0,)), ((), ())), preferred_element_type=F32
        )
        return (
            lax.psum_scatter(whole, ("tm", "dp"), scatter_dimension=0, tiled=True) * scale_factor
        )
    block = hid // (count * sides)
    half = (2 * count, block, channels)
    quarter = (count, block, channels)
    keep, send = call(
        weight_grad,
        [struct(half, F32), struct(half, BF16)],
        [pltpu.VMEM((4 * count, block, channels), F32)],
        d_pre,
        scaled,
        flops=2 * hid * channels * d_pre.shape[0],
    )
    got = lax.ppermute(send, "dp", [(i, i ^ 1) for i in range(4)])
    keep, send = call(fold_pair, [struct(quarter, F32), struct(quarter, BF16)], [], keep, got)
    got = lax.ppermute(send, "dp", [(i, i ^ 2) for i in range(4)])
    piece = (block, channels)
    keep, *sends = call(
        functools.partial(fold_tm, count),
        [struct(piece, F32)] + [struct(piece, BF16)] * (count - 1),
        [],
        keep,
        got,
    )
    got = exchange([keep] + list(sends))[1:]
    return call(
        functools.partial(fold_last, scale_factor), [struct(piece, F32)], [], keep, *got
    )[0]


def local(clips, cotangent, spatial_kernel, temporal_kernel, norm_gain, w_expand, w_project):
    _, frames, height, width, channels = clips.shape
    members = lax.axis_size("tm")
    device_count = members * lax.axis_size("dp")
    pixels = height * width
    scale_factor = float(clips.shape[0] * frames * pixels * device_count) ** (-0.5)
    hid = w_expand.shape[1]
    chunk = 256
    blocks = channels // LANES
    count = members if members <= 8 and height % members == 0 else 1
    all_frames = frames * members
    columns = pixels // members
    tokens = all_frames * columns

    def to_columns(pieces):
        if count > 1:
            return exchange(pieces)
        whole = pieces[0][None]
        return [lax.all_to_all(whole, "tm", split_axis=2, concat_axis=1, tiled=True)[0]]

    def to_frames(pieces):
        if count > 1:
            return exchange(pieces)
        whole = pieces[0][None]
        return [lax.all_to_all(whole, "tm", split_axis=1, concat_axis=2, tiled=True)[0]]

    kernel = spatial_kernel.reshape(spatial_kernel.shape[:2] + (blocks, LANES)).transpose(2, 0, 1, 3)
    gain = norm_gain.reshape(1, channels)
    pad = pltpu.VMEM((blocks, frames, height, width + 2 * PAD, LANES), F32)
    conv_flops = 2 * 49 * frames * pixels * channels
    mlp_flops = 2 * tokens * channels * hid

    piece = struct((frames, pixels // count, channels), BF16)
    outs = call(
        functools.partial(spatial_fwd, count),
        [piece] * (2 * count),
        [pad, pltpu.VMEM((frames, height, width, channels), F32)],
        clips,
        cotangent,
        kernel,
        flops=conv_flops,
    )
    firsts = to_columns(list(outs[:count]))
    cots = to_columns(list(outs[count:]))

    column = (all_frames, columns, channels)
    back = struct((all_frames // count, columns, channels), BF16)
    outs = call(
        functools.partial(mlp_fwd, count, chunk),
        [back] * count
        + [
            struct((tokens, channels), BF16),
            struct((tokens, hid), BF16),
            struct((tokens, channels), F32),
            struct((tokens, 1), F32),
        ],
        [
            pltpu.VMEM(column, F32),
            pltpu.VMEM(column, F32),
            pltpu.VMEM((tokens, hid), BF16),
            pltpu.VMEM(column, F32),
        ],
        *firsts,
        temporal_kernel,
        gain,
        w_expand,
        w_project,
        flops=2 * mlp_flops,
    )
    scaled, slope, normed, inv_std = outs[count:]
    branches = to_frames(list(outs[:count]))

    outs = call(
        functools.partial(mlp_bwd, count, chunk),
        [back] * count + [struct((tokens, hid), BF16)],
        [pltpu.VMEM(column, F32), pltpu.VMEM(column, F32), pltpu.VMEM(column, F32)],
        *cots,
        slope,
        normed,
        inv_std,
        temporal_kernel,
        gain,
        w_expand,
        w_project,
        flops=2 * mlp_flops,
    )
    d_pre = outs[count]
    d_firsts = to_frames(list(outs[:count]))

    grad_expand = scatter_grad(d_pre, scaled, count, scale_factor)

    grad_clips = call(
        functools.partial(spatial_bwd, count),
        [struct(clips.shape, BF16)],
        [pad],
        *d_firsts,
        cotangent,
        kernel,
        flops=conv_flops,
    )[0]
    block_out = call(
        functools.partial(add_residual, count), [struct(clips.shape, BF16)], [], *branches, clips
    )[0]
    return (block_out, grad_clips, grad_expand)


def solution(mesh):
    in_specs = (
        P(("groups", "dp"), "tm", None, None, None),
        P(("groups", "dp"), "tm", None, None, None),
        P(),
        P(),
        P(),
        P(),
        P(),
    )
    out_specs = (
        P(("groups", "dp"), "tm", None, None, None),
        P(("groups", "dp"), "tm", None, None, None),
        P(("groups", "tm", "dp"), None),
    )
    return jax.shard_map(local, mesh=mesh, in_specs=in_specs, out_specs=out_specs, check_vma=False)
```

```python
import functools
import jax
import jax.numpy as jnp
from jax import lax
from jax.experimental import pallas as pl
from jax.experimental.pallas import tpu as pltpu
from jax.sharding import PartitionSpec as P

LANES = 128
PAD = 8
F32 = jnp.float32
BF16 = jnp.bfloat16
VMEM_LIMIT = 32 * 1024 * 1024


def call(body, outs, scratch, *args, cost=0, far=0, wait=(), limit=VMEM_LIMIT):
    specs = [pl.BlockSpec(memory_space=pltpu.HBM)] * far
    specs += [pl.BlockSpec(memory_space=pltpu.VMEM)] * (len(args) - far)
    args = [
        pltpu.with_memory_space_constraint(a, pltpu.HBM) if i < far else a
        for i, a in enumerate(args)
    ]
    given = len(args)
    for a in wait:
        specs.append(pl.BlockSpec(memory_space=pl.ANY))
        args.append(pltpu.with_memory_space_constraint(a, pltpu.HBM) if a.ndim == 5 else a)

    def kernel(*refs):
        body(*refs[:given], *refs[given + len(wait) :])

    return pl.pallas_call(
        kernel,
        out_shape=tuple(outs),
        in_specs=specs,
        out_specs=tuple([pl.BlockSpec(memory_space=pltpu.VMEM)] * len(outs)),
        scratch_shapes=list(scratch),
        cost_estimate=pl.CostEstimate(flops=cost, bytes_accessed=cost, transcendentals=0),
        compiler_params=pltpu.CompilerParams(vmem_limit_bytes=limit),
    )(*args)


def struct(shape, dtype):
    return jax.ShapeDtypeStruct(tuple(shape), dtype)


def slot_to(step, count):
    if count == 1:
        return 0
    return lax.rem(lax.axis_index("tm") + step, count)


def slot_from(step, count):
    if count == 1:
        return 0
    return lax.rem(lax.axis_index("tm") + count - step, count)


def exchange(pieces):
    count = len(pieces)
    got = [pieces[0]]
    for step in range(1, count):
        pairs = [(i, (i + step) % count) for i in range(count)]
        got.append(lax.ppermute(pieces[step], "tm", pairs))
    return got


def conv_rows(pad_ref, kernel_ref, block, col, height, flip, emit):
    taps = kernel_ref.shape[0]
    lanes = slice(block * LANES, (block + 1) * LANES)
    radius = taps // 2
    acc = [None] * height
    for col_off in range(taps):
        shift = radius - col_off if flip else col_off - radius
        weights = [
            kernel_ref[row_off, pl.ds(col_off, 1), lanes] for row_off in range(taps)
        ]
        for row in range(height):
            values = pad_ref[block, :, row, pl.ds(PAD + col + shift, 8), :]
            for row_off in range(taps):
                out = row - radius + row_off if flip else row + radius - row_off
                if 0 <= out < height:
                    term = values * weights[row_off][None]
                    acc[out] = term if acc[out] is None else acc[out] + term
    for row in range(height):
        emit(row, acc[row])


def clear_pads(pad_ref, width):
    blocks, frames, height, _, lanes = pad_ref.shape
    zero = jnp.zeros((blocks, frames, height, PAD, lanes), F32)
    pad_ref[:, :, :, 0:PAD, :] = zero
    pad_ref[:, :, :, PAD + width : PAD + width + PAD, :] = zero


def spatial_fwd(count, *refs):
    clips_far, cot_far, kernel_far = refs[:3]
    held = (len(refs) - 3 - 2 * count - 5) // 2
    fars = refs[3 : 3 + held]
    refs = refs[3 + held :]
    firsts = refs[:count]
    cots = refs[count : 2 * count]
    nears = refs[2 * count : 2 * count + held]
    clips, kernel, pad_ref, flat, sems = refs[2 * count + held :]
    frames, height, width, channels = clips.shape
    blocks = channels // LANES
    pixels = height * width // count
    rows = height // count
    copies = [
        pltpu.make_async_copy(clips_far.at[0], clips, sems.at[0]),
        pltpu.make_async_copy(kernel_far, kernel, sems.at[1]),
    ]
    for step in range(count):
        base = slot_to(step, count) * rows
        copies.append(
            pltpu.make_async_copy(
                cot_far.at[0, :, pl.ds(base, rows)], cots[step], sems.at[2 + step]
            )
        )
    for index in range(held):
        copies.append(
            pltpu.make_async_copy(fars[index], nears[index], sems.at[2 + count + index])
        )
    for copy in copies:
        copy.start()
    clear_pads(pad_ref, width)
    copies[0].wait()
    for block in range(blocks):
        lanes = slice(block * LANES, (block + 1) * LANES)
        pad_ref[block, :, :, PAD : PAD + width, :] = clips[:, :, :, lanes].astype(F32)
    copies[1].wait()
    for block in range(blocks):
        lanes = slice(block * LANES, (block + 1) * LANES)
        for col in range(0, width, 8):

            def emit(row, value):
                flat[:, row, pl.ds(col, 8), lanes] = value

            conv_rows(pad_ref, kernel, block, col, height, False, emit)
    for step in range(count):
        base = slot_to(step, count) * rows
        firsts[step][...] = (
            flat[:, pl.ds(base, rows), :, :].reshape(frames, pixels, channels).astype(BF16)
        )
    for copy in copies[2:]:
        copy.wait()


def spatial_bwd(count, *refs):
    pieces = refs[:count]
    cot, kernel, out_ref, pad_ref = refs[count:]
    _, frames, height, width, channels = cot.shape
    blocks = channels // LANES
    rows = height // count
    clear_pads(pad_ref, width)
    for step in range(count):
        base = slot_from(step, count) * rows
        for block in range(blocks):
            lanes = slice(block * LANES, (block + 1) * LANES)
            piece = pieces[step][:, :, lanes].astype(F32).reshape(frames, rows, width, LANES)
            pad_ref[block, :, pl.ds(base, rows), PAD : PAD + width, :] = piece
    for block in range(blocks):
        lanes = slice(block * LANES, (block + 1) * LANES)
        for col in range(0, width, 16):
            halves = []
            for part in range(2):
                rows_out = []
                conv_rows(
                    pad_ref, kernel, block, col + 8 * part, height, True,
                    lambda row, value: rows_out.append(value),
                )
                halves.append(rows_out)
            for row in range(height):
                total = jnp.concatenate([halves[0][row], halves[1][row]], axis=1)
                total = total + cot[0, :, row, pl.ds(col, 16), lanes].astype(F32)
                out_ref[0, :, row, pl.ds(col, 16), lanes] = total.astype(BF16)


def mix_frames(source, target, kernel, flip):
    frames = source.shape[0]
    taps = kernel.shape[0]
    radius = taps // 2
    if frames <= 16:
        for out in range(frames):
            total = None
            for inp in range(frames):
                lag = (out - inp if flip else inp - out) + radius
                if 0 <= lag < taps:
                    term = kernel[pl.ds(lag, 1), :] * source[inp]
                    total = term if total is None else total + term
            target[out] = total.astype(BF16).astype(F32)
        return

    def one(out, carry):
        def tap(inp, total):
            lag = (out - inp if flip else inp - out) + radius
            return total + kernel[pl.ds(lag, 1), :] * source[inp]

        low = jnp.maximum(out - radius, 0)
        high = jnp.minimum(out + radius + 1, frames)
        total = lax.fori_loop(low, high, tap, jnp.zeros(source.shape[1:], F32))
        target[out] = total.astype(BF16).astype(F32)
        return carry

    lax.fori_loop(0, frames, one, 0)


def place_frames(count, pieces, target):
    for step in range(count):
        frames = pieces[step].shape[0]
        base = slot_from(step, count) * frames
        piece = pieces[step][...].reshape((frames,) + target.shape[1:])
        target[pl.ds(base, frames)] = piece.astype(target.dtype)


def mlp_fwd(count, chunk, *refs):
    pieces = refs[:count]
    taps, gain, w_expand, w_project = refs[count : count + 4]
    branches = refs[count + 4 : 2 * count + 4]
    scaled, slope, normed, inv_std, mixed_in, mixed, hidden, branch = refs[2 * count + 4 :]
    frames, pixels, channels = mixed_in.shape
    tokens = frames * pixels
    place_frames(count, pieces, mixed_in)
    mix_frames(mixed_in, mixed, taps, False)
    values = mixed[...].reshape(tokens, channels)
    average = jnp.mean(values, axis=-1, keepdims=True)
    centred = values - average
    inverse = lax.rsqrt(jnp.mean(centred * centred, axis=-1, keepdims=True) + 1e-06)
    inv_std[...] = inverse
    norm = centred * inverse
    normed[...] = norm
    scaled[...] = (norm * gain[...].reshape(1, channels)).astype(BF16)
    for start in range(0, w_expand.shape[1], chunk):
        part = slice(start, start + chunk)
        pre = jnp.dot(scaled[...], w_expand[:, part], preferred_element_type=F32)
        cdf = 0.5 + 0.5 * lax.erf(pre * 0.7071067811865476)
        hidden[:, part] = (pre * cdf).astype(BF16)
        slope[:, part] = (cdf + pre * jnp.exp(-0.5 * pre * pre) * 0.3989422804014327).astype(BF16)
    branch[...] = jnp.dot(hidden[...], w_project[...], preferred_element_type=F32).reshape(
        frames, pixels, channels
    )
    own = frames // count
    for step in range(count):
        base = slot_to(step, count) * own
        branches[step][...] = branch[pl.ds(base, own)].astype(BF16)


def hidden_bwd(count, chunk, with_grad, *refs):
    pieces = refs[:count]
    slope, w_project, scaled, d_pre = refs[count : count + 4]
    grads = refs[-1]
    frames, pixels, channels = grads.shape
    tokens = frames * pixels
    place_frames(count, pieces, grads)
    grad_rows = grads[...].reshape(tokens, channels).astype(BF16)
    last = (((1,), (1,)), ((), ()))
    for start in range(0, w_project.shape[0], chunk):
        part = slice(start, start + chunk)
        d_hidden = lax.dot_general(grad_rows, w_project[part, :], last, preferred_element_type=F32)
        d_pre[:, part] = (d_hidden * slope[:, part].astype(F32)).astype(BF16)
    if with_grad:
        keep, send, full = refs[count + 4 : count + 7]
        full[...] = lax.dot_general(
            d_pre[...], scaled[...], (((0,), (0,)), ((), ())), preferred_element_type=F32
        ).reshape(full.shape)
        core = lax.rem(lax.axis_index("dp"), 2)
        for pair in range(full.shape[0] // 2):
            keep[pair] = full[2 * pair + core]
            send[pair] = full[2 * pair + 1 - core].astype(BF16)


def token_bwd(count, *refs):
    d_pre, normed, inv_std, taps, gain, w_expand = refs[:6]
    outs = refs[6 : count + 6]
    d_second, d_first = refs[count + 6 :]
    frames, pixels, channels = d_second.shape
    last = (((1,), (1,)), ((), ()))
    d_scaled = lax.dot_general(d_pre[...], w_expand[...], last, preferred_element_type=F32)
    d_normed = d_scaled * gain[...].reshape(1, channels)
    norm = normed[...]
    d_tokens = inv_std[...] * (
        d_normed
        - jnp.mean(d_normed, axis=-1, keepdims=True)
        - norm * jnp.mean(d_normed * norm, axis=-1, keepdims=True)
    )
    d_second[...] = d_tokens.astype(BF16).astype(F32).reshape(frames, pixels, channels)
    mix_frames(d_second, d_first, taps, True)
    own = frames // count
    for step in range(count):
        base = slot_to(step, count) * own
        outs[step][...] = d_first[pl.ds(base, own)].astype(BF16)


def add_residual(count, *refs):
    pieces = refs[:count]
    clips, out_ref = refs[count:]
    _, frames, height, width, channels = clips.shape
    rows = height // count
    for step in range(count):
        base = slot_from(step, count) * rows
        piece = pieces[step][...].reshape(frames, rows, width, channels).astype(F32)
        here = (0, slice(None), pl.ds(base, rows))
        out_ref[here] = (clips[here].astype(F32) + piece).astype(BF16)


def fold_pair(keep_in, got, keep, send):
    side = lax.div(lax.axis_index("dp"), 2)
    for slot in range(keep.shape[0]):
        mine, other = 2 * slot + side, 2 * slot + 1 - side
        keep[slot] = keep_in[mine] + got[mine].astype(F32)
        send[slot] = (keep_in[other] + got[other].astype(F32)).astype(BF16)


def fold_near(keep_in, got, keep, *sends):
    me = lax.axis_index("tm")
    for far in range(2):
        mine = lax.bitwise_xor(me, 2 * far)
        other = lax.bitwise_xor(me, 2 * far + 1)
        keep[far] = keep_in[mine] + got[mine].astype(F32)
        sends[far][...] = (keep_in[other] + got[other].astype(F32)).astype(BF16)


def fold_far(keep_in, got, got_far, keep, send):
    keep[...] = keep_in[0] + got[...].astype(F32)
    send[...] = (keep_in[1] + got_far[...].astype(F32)).astype(BF16)


def fold_last(scale_factor, keep_in, *refs):
    total = keep_in[...]
    for got in refs[:-1]:
        total = total + got[...].astype(F32)
    refs[-1][...] = total * scale_factor


def scatter_grad(keep, send, count, scale_factor, d_first, grad_clips):
    channels = keep.shape[-1]
    block = keep.shape[1]
    quarter = (count, block, channels)
    piece = (block, channels)
    got = lax.ppermute(send, "dp", [(i, i ^ 1) for i in range(4)])
    keep, send = call(
        fold_pair, [struct(quarter, F32), struct(quarter, BF16)], [], keep, got, wait=[d_first]
    )
    got = lax.ppermute(send, "dp", [(i, i ^ 2) for i in range(4)])
    pair = (2,) + piece
    keep, *sends = call(
        fold_near, [struct(pair, F32), struct(piece, BF16), struct(piece, BF16)], [], keep, got
    )
    near = [lax.ppermute(send, "tm", [(i, i ^ 1) for i in range(4)]) for send in sends]
    keep, send = call(
        fold_far, [struct(piece, F32), struct(piece, BF16)], [], keep, *near, wait=[grad_clips]
    )
    got = lax.ppermute(send, "tm", [(i, i ^ 2) for i in range(4)])
    return call(functools.partial(fold_last, scale_factor), [struct(piece, F32)], [], keep, got)[0]


def local(clips, cotangent, spatial_kernel, temporal_kernel, norm_gain, w_expand, w_project):
    _, frames, height, width, channels = clips.shape
    members = lax.axis_size("tm")
    device_count = members * lax.axis_size("dp")
    pixels = height * width
    scale_factor = float(clips.shape[0] * frames * pixels * device_count) ** (-0.5)
    hid = w_expand.shape[1]
    chunk = 256
    blocks = channels // LANES
    count = members if members <= 8 and height % members == 0 else 1
    all_frames = frames * members
    columns = pixels // members
    tokens = all_frames * columns

    def to_columns(pieces):
        if count > 1:
            return exchange(pieces)
        whole = pieces[0].reshape(1, frames, pixels, channels)
        return [lax.all_to_all(whole, "tm", split_axis=2, concat_axis=1, tiled=True)[0]]

    def to_frames(pieces):
        if count > 1:
            return exchange(pieces)
        whole = pieces[0][None]
        return [lax.all_to_all(whole, "tm", split_axis=1, concat_axis=2, tiled=True)[0]]

    pad = pltpu.VMEM((blocks, frames, height, width + 2 * PAD, LANES), F32)
    piece = struct((frames, pixels // count, channels), BF16)
    cot_piece = struct((frames, height // count, width, channels), BF16)
    held = [temporal_kernel, w_expand, w_project]
    outs = call(
        functools.partial(spatial_fwd, count),
        [piece] * count + [cot_piece] * count + [struct(a.shape, a.dtype) for a in held],
        [
            pltpu.VMEM(clips.shape[1:], BF16),
            pltpu.VMEM(spatial_kernel.shape, F32),
            pad,
            pltpu.VMEM((frames, height, width, channels), F32),
            pltpu.SemaphoreType.DMA((2 + count + len(held),)),
        ],
        clips,
        cotangent,
        spatial_kernel,
        *held,
        far=3 + len(held),
    )
    firsts = to_columns(list(outs[:count]))
    cots = to_columns(list(outs[count : 2 * count]))
    temporal_kernel, w_expand, w_project = outs[2 * count :]

    column = (all_frames, columns, channels)
    back = struct((all_frames // count, columns, channels), BF16)
    outs = call(
        functools.partial(mlp_fwd, count, chunk),
        [back] * count
        + [
            struct((tokens, channels), BF16),
            struct((tokens, hid), BF16),
            struct((tokens, channels), F32),
            struct((tokens, 1), F32),
        ],
        [
            pltpu.VMEM(column, F32),
            pltpu.VMEM(column, F32),
            pltpu.VMEM((tokens, hid), BF16),
            pltpu.VMEM(column, F32),
        ],
        *firsts,
        temporal_kernel,
        norm_gain,
        w_expand,
        w_project,
    )
    scaled, slope, normed, inv_std = outs[count:]
    branches = to_frames(list(outs[:count]))

    sides = lax.axis_size("dp")
    staged = count == 4 and sides == 4
    half = (2 * count, hid // (sides * count), channels)
    outs = call(
        functools.partial(hidden_bwd, count, chunk, staged),
        [struct((tokens, hid), BF16)] + [struct(half, F32), struct(half, BF16)] * staged,
        [pltpu.VMEM((2 * half[0],) + half[1:], F32)] * staged + [pltpu.VMEM(column, F32)],
        *cots,
        slope,
        w_project,
        scaled,
    )
    d_pre = outs[0]
    shares = outs[1:]
    outs = call(
        functools.partial(token_bwd, count),
        [back] * count,
        [pltpu.VMEM(column, F32), pltpu.VMEM(column, F32)],
        d_pre,
        normed,
        inv_std,
        temporal_kernel,
        norm_gain,
        w_expand,
    )
    d_firsts = to_frames(list(outs))

    block_out = call(
        functools.partial(add_residual, count), [struct(clips.shape, BF16)], [], *branches, clips
    )[0]
    grad_clips = call(
        functools.partial(spatial_bwd, count),
        [struct(clips.shape, BF16)],
        [pad],
        *d_firsts,
        cotangent,
        spatial_kernel,
    )[0]
    if staged:
        grad_expand = scatter_grad(*shares, count, scale_factor, outs[0], grad_clips)
    else:
        whole = lax.dot_general(
            d_pre, scaled, (((0,), (0,)), ((), ())), preferred_element_type=F32
        )
        whole = lax.psum_scatter(whole, ("tm", "dp"), scatter_dimension=0, tiled=True)
        grad_expand = whole * scale_factor
    return (block_out, grad_clips, grad_expand)


def solution(mesh):
    in_specs = (
        P(("groups", "dp"), "tm", None, None, None),
        P(("groups", "dp"), "tm", None, None, None),
        P(),
        P(),
        P(),
        P(),
        P(),
    )
    out_specs = (
        P(("groups", "dp"), "tm", None, None, None),
        P(("groups", "dp"), "tm", None, None, None),
        P(("groups", "tm", "dp"), None),
    )
    return jax.shard_map(local, mesh=mesh, in_specs=in_specs, out_specs=out_specs, check_vma=False)
```

```python
import functools
import jax
import jax.numpy as jnp
from jax import lax
from jax.experimental import pallas as pl
from jax.experimental.pallas import tpu as pltpu
from jax.sharding import PartitionSpec as P

LANES = 128
PAD = 8
F32 = jnp.float32
BF16 = jnp.bfloat16
VMEM_LIMIT = 32 * 1024 * 1024


def call(body, outs, scratch, *args, cost=0, far=0, wait=(), limit=VMEM_LIMIT):
    specs = [pl.BlockSpec(memory_space=pltpu.HBM)] * far
    specs += [pl.BlockSpec(memory_space=pltpu.VMEM)] * (len(args) - far)
    args = [
        pltpu.with_memory_space_constraint(a, pltpu.HBM) if i < far else a
        for i, a in enumerate(args)
    ]
    given = len(args)
    for a in wait:
        specs.append(pl.BlockSpec(memory_space=pl.ANY))
        args.append(pltpu.with_memory_space_constraint(a, pltpu.HBM) if a.ndim == 5 else a)

    def kernel(*refs):
        body(*refs[:given], *refs[given + len(wait) :])

    return pl.pallas_call(
        kernel,
        out_shape=tuple(outs),
        in_specs=specs,
        out_specs=tuple([pl.BlockSpec(memory_space=pltpu.VMEM)] * len(outs)),
        scratch_shapes=list(scratch),
        cost_estimate=pl.CostEstimate(flops=cost, bytes_accessed=cost, transcendentals=0),
        compiler_params=pltpu.CompilerParams(vmem_limit_bytes=limit),
    )(*args)


def struct(shape, dtype):
    return jax.ShapeDtypeStruct(tuple(shape), dtype)


def slot_to(step, count):
    if count == 1:
        return 0
    return lax.rem(lax.axis_index("tm") + step, count)


def slot_from(step, count):
    if count == 1:
        return 0
    return lax.rem(lax.axis_index("tm") + count - step, count)


def partner(step, count):
    if count == 1:
        return 0
    return lax.bitwise_xor(lax.axis_index("tm"), step)


def swap(pieces):
    got = [pieces[0]]
    for step in range(1, len(pieces)):
        pairs = [(i, i ^ step) for i in range(len(pieces))]
        got.append(lax.ppermute(pieces[step], "tm", pairs))
    return got


def exchange(pieces):
    count = len(pieces)
    got = [pieces[0]]
    for step in range(1, count):
        pairs = [(i, (i + step) % count) for i in range(count)]
        got.append(lax.ppermute(pieces[step], "tm", pairs))
    return got


def conv_rows(pad_ref, kernel_ref, block, col, height, flip, emit):
    taps = kernel_ref.shape[0]
    lanes = slice(block * LANES, (block + 1) * LANES)
    radius = taps // 2
    acc = [None] * height
    for col_off in range(taps):
        shift = radius - col_off if flip else col_off - radius
        weights = [
            kernel_ref[row_off, pl.ds(col_off, 1), lanes] for row_off in range(taps)
        ]
        for row in range(height):
            values = pad_ref[block, :, row, pl.ds(PAD + col + shift, 8), :]
            for row_off in range(taps):
                out = row - radius + row_off if flip else row + radius - row_off
                if 0 <= out < height:
                    term = values * weights[row_off][None]
                    acc[out] = term if acc[out] is None else acc[out] + term
    for row in range(height):
        emit(row, acc[row])


def clear_pads(pad_ref, width):
    blocks, frames, height, _, lanes = pad_ref.shape
    zero = jnp.zeros((blocks, frames, height, PAD, lanes), F32)
    pad_ref[:, :, :, 0:PAD, :] = zero
    pad_ref[:, :, :, PAD + width : PAD + width + PAD, :] = zero


def spatial_fwd(count, *refs):
    clips_far, cot_far, kernel_far = refs[:3]
    held = (len(refs) - 3 - 2 * count - 5) // 2
    fars = refs[3 : 3 + held]
    refs = refs[3 + held :]
    firsts = refs[:count]
    cots = refs[count : 2 * count]
    nears = refs[2 * count : 2 * count + held]
    clips, kernel, pad_ref, flat, sems = refs[2 * count + held :]
    frames, height, width, channels = clips.shape
    blocks = channels // LANES
    pixels = height * width // count
    rows = height // count
    copies = [
        pltpu.make_async_copy(clips_far.at[0], clips, sems.at[0]),
        pltpu.make_async_copy(kernel_far, kernel, sems.at[1]),
    ]
    for step in range(count):
        base = slot_to(step, count) * rows
        copies.append(
            pltpu.make_async_copy(
                cot_far.at[0, :, pl.ds(base, rows)], cots[step], sems.at[2 + step]
            )
        )
    for index in range(held):
        copies.append(
            pltpu.make_async_copy(fars[index], nears[index], sems.at[2 + count + index])
        )
    for copy in copies:
        copy.start()
    clear_pads(pad_ref, width)
    copies[0].wait()
    for block in range(blocks):
        lanes = slice(block * LANES, (block + 1) * LANES)
        pad_ref[block, :, :, PAD : PAD + width, :] = clips[:, :, :, lanes].astype(F32)
    copies[1].wait()
    for block in range(blocks):
        lanes = slice(block * LANES, (block + 1) * LANES)
        for col in range(0, width, 8):

            def emit(row, value):
                flat[:, row, pl.ds(col, 8), lanes] = value

            conv_rows(pad_ref, kernel, block, col, height, False, emit)
    for step in range(count):
        base = slot_to(step, count) * rows
        firsts[step][...] = (
            flat[:, pl.ds(base, rows), :, :].reshape(frames, pixels, channels).astype(BF16)
        )
    for copy in copies[2:]:
        copy.wait()


def spatial_bwd(count, *refs):
    pieces = refs[:count]
    clips, cot, kernel, block_out, out_ref, pad_ref = refs[count:]
    _, frames, height, width, channels = cot.shape
    blocks = channels // LANES
    rows = height // count
    clear_pads(pad_ref, width)
    for step in range(count):
        base = partner(step, count) * rows
        for block in range(blocks):
            lanes = slice(block * LANES, (block + 1) * LANES)
            piece = pieces[step][1, :, :, lanes].astype(F32).reshape(frames, rows, width, LANES)
            pad_ref[block, :, pl.ds(base, rows), PAD : PAD + width, :] = piece
        here = (0, slice(None), pl.ds(base, rows))
        branch = pieces[step][0].reshape(frames, rows, width, channels).astype(F32)
        block_out[here] = (clips[here].astype(F32) + branch).astype(BF16)
    for block in range(blocks):
        lanes = slice(block * LANES, (block + 1) * LANES)
        for col in range(0, width, 16):
            halves = []
            for part in range(2):
                rows_out = []
                conv_rows(
                    pad_ref, kernel, block, col + 8 * part, height, True,
                    lambda row, value: rows_out.append(value),
                )
                halves.append(rows_out)
            for row in range(height):
                total = jnp.concatenate([halves[0][row], halves[1][row]], axis=1)
                total = total + cot[0, :, row, pl.ds(col, 16), lanes].astype(F32)
                out_ref[0, :, row, pl.ds(col, 16), lanes] = total.astype(BF16)


def mix_frames(source, target, kernel, flip):
    frames = source.shape[0]
    taps = kernel.shape[0]
    radius = taps // 2
    if frames <= 16:
        for out in range(frames):
            total = None
            for inp in range(frames):
                lag = (out - inp if flip else inp - out) + radius
                if 0 <= lag < taps:
                    term = kernel[pl.ds(lag, 1), :] * source[inp]
                    total = term if total is None else total + term
            target[out] = total.astype(BF16).astype(F32)
        return

    def one(out, carry):
        def tap(inp, total):
            lag = (out - inp if flip else inp - out) + radius
            return total + kernel[pl.ds(lag, 1), :] * source[inp]

        low = jnp.maximum(out - radius, 0)
        high = jnp.minimum(out + radius + 1, frames)
        total = lax.fori_loop(low, high, tap, jnp.zeros(source.shape[1:], F32))
        target[out] = total.astype(BF16).astype(F32)
        return carry

    lax.fori_loop(0, frames, one, 0)


def place_frames(count, pieces, target):
    for step in range(count):
        frames = pieces[step].shape[0]
        base = slot_from(step, count) * frames
        piece = pieces[step][...].reshape((frames,) + target.shape[1:])
        target[pl.ds(base, frames)] = piece.astype(target.dtype)


def mlp_fwd(count, chunk, *refs):
    pieces = refs[:count]
    taps, gain, w_expand, w_project = refs[count : count + 4]
    branch, scaled, slope, normed, inv_std, mixed_in, mixed, hidden = refs[count + 4 :]
    frames, pixels, channels = mixed_in.shape
    tokens = frames * pixels
    place_frames(count, pieces, mixed_in)
    mix_frames(mixed_in, mixed, taps, False)
    values = mixed[...].reshape(tokens, channels)
    average = jnp.mean(values, axis=-1, keepdims=True)
    centred = values - average
    inverse = lax.rsqrt(jnp.mean(centred * centred, axis=-1, keepdims=True) + 1e-06)
    inv_std[...] = inverse
    norm = centred * inverse
    normed[...] = norm
    scaled[...] = (norm * gain[...].reshape(1, channels)).astype(BF16)
    for start in range(0, w_expand.shape[1], chunk):
        part = slice(start, start + chunk)
        pre = jnp.dot(scaled[...], w_expand[:, part], preferred_element_type=F32)
        cdf = 0.5 + 0.5 * lax.erf(pre * 0.7071067811865476)
        hidden[:, part] = (pre * cdf).astype(BF16)
        slope[:, part] = (cdf + pre * jnp.exp(-0.5 * pre * pre) * 0.3989422804014327).astype(BF16)
    out = jnp.dot(hidden[...], w_project[...], preferred_element_type=F32).astype(BF16)
    branch[...] = out.reshape(branch.shape)


def hidden_bwd(count, chunk, with_grad, *refs):
    pieces = refs[:count]
    slope, w_project, scaled, d_pre = refs[count : count + 4]
    grads = refs[-1]
    frames, pixels, channels = grads.shape
    tokens = frames * pixels
    place_frames(count, pieces, grads)
    grad_rows = grads[...].reshape(tokens, channels).astype(BF16)
    last = (((1,), (1,)), ((), ()))
    for start in range(0, w_project.shape[0], chunk):
        part = slice(start, start + chunk)
        d_hidden = lax.dot_general(grad_rows, w_project[part, :], last, preferred_element_type=F32)
        d_pre[:, part] = (d_hidden * slope[:, part].astype(F32)).astype(BF16)
    if with_grad:
        keep, send, full = refs[count + 4 : count + 7]
        full[...] = lax.dot_general(
            d_pre[...], scaled[...], (((0,), (0,)), ((), ())), preferred_element_type=F32
        ).reshape(full.shape)
        core = lax.rem(lax.axis_index("dp"), 2)
        for pair in range(full.shape[0] // 2):
            keep[pair] = full[2 * pair + core]
            send[pair] = full[2 * pair + 1 - core].astype(BF16)


def token_bwd(count, *refs):
    d_pre, normed, inv_std, taps, gain, w_expand, branch = refs[:7]
    outs = refs[7 : count + 7]
    d_second, d_first = refs[count + 7 :]
    frames, pixels, channels = d_second.shape
    last = (((1,), (1,)), ((), ()))
    d_scaled = lax.dot_general(d_pre[...], w_expand[...], last, preferred_element_type=F32)
    d_normed = d_scaled * gain[...].reshape(1, channels)
    norm = normed[...]
    d_tokens = inv_std[...] * (
        d_normed
        - jnp.mean(d_normed, axis=-1, keepdims=True)
        - norm * jnp.mean(d_normed * norm, axis=-1, keepdims=True)
    )
    d_second[...] = d_tokens.astype(BF16).astype(F32).reshape(frames, pixels, channels)
    mix_frames(d_second, d_first, taps, True)
    own = frames // count
    for step in range(count):
        base = partner(step, count) * own
        outs[step][0] = branch[pl.ds(base, own)]
        outs[step][1] = d_first[pl.ds(base, own)].astype(BF16)


def fold_pair(keep_in, got, keep, send):
    side = lax.div(lax.axis_index("dp"), 2)
    for slot in range(keep.shape[0]):
        mine, other = 2 * slot + side, 2 * slot + 1 - side
        keep[slot] = keep_in[mine] + got[mine].astype(F32)
        send[slot] = (keep_in[other] + got[other].astype(F32)).astype(BF16)


def fold_near(keep_in, got, keep, *sends):
    me = lax.axis_index("tm")
    for far in range(2):
        mine = lax.bitwise_xor(me, 2 * far)
        other = lax.bitwise_xor(me, 2 * far + 1)
        keep[far] = keep_in[mine] + got[mine].astype(F32)
        sends[far][...] = (keep_in[other] + got[other].astype(F32)).astype(BF16)


def fold_far(keep_in, got, got_far, keep, send):
    keep[...] = keep_in[0] + got[...].astype(F32)
    send[...] = (keep_in[1] + got_far[...].astype(F32)).astype(BF16)


def fold_last(scale_factor, keep_in, *refs):
    total = keep_in[...]
    for got in refs[:-1]:
        total = total + got[...].astype(F32)
    refs[-1][...] = total * scale_factor


def scatter_grad(keep, send, count, scale_factor, d_first):
    channels = keep.shape[-1]
    block = keep.shape[1]
    quarter = (count, block, channels)
    piece = (block, channels)
    got = lax.ppermute(send, "dp", [(i, i ^ 1) for i in range(4)])
    keep, send = call(
        fold_pair, [struct(quarter, F32), struct(quarter, BF16)], [], keep, got, wait=[d_first]
    )
    got = lax.ppermute(send, "dp", [(i, i ^ 2) for i in range(4)])
    pair = (2,) + piece
    keep, *sends = call(
        fold_near, [struct(pair, F32), struct(piece, BF16), struct(piece, BF16)], [], keep, got
    )
    near = [lax.ppermute(send, "tm", [(i, i ^ 1) for i in range(4)]) for send in sends]
    keep, send = call(
        fold_far, [struct(piece, F32), struct(piece, BF16)], [], keep, *near
    )
    got = lax.ppermute(send, "tm", [(i, i ^ 2) for i in range(4)])
    return call(functools.partial(fold_last, scale_factor), [struct(piece, F32)], [], keep, got)[0]


def local(clips, cotangent, spatial_kernel, temporal_kernel, norm_gain, w_expand, w_project):
    _, frames, height, width, channels = clips.shape
    members = lax.axis_size("tm")
    device_count = members * lax.axis_size("dp")
    pixels = height * width
    scale_factor = float(clips.shape[0] * frames * pixels * device_count) ** (-0.5)
    hid = w_expand.shape[1]
    chunk = 256
    blocks = channels // LANES
    count = members if members in (2, 4, 8) and height % members == 0 else 1
    all_frames = frames * members
    columns = pixels // members
    tokens = all_frames * columns

    def to_columns(pieces):
        if count > 1:
            return exchange(pieces)
        whole = pieces[0].reshape(1, frames, pixels, channels)
        return [lax.all_to_all(whole, "tm", split_axis=2, concat_axis=1, tiled=True)[0]]

    def to_frames(pieces):
        if count > 1:
            return swap(pieces)
        return [lax.all_to_all(pieces[0], "tm", split_axis=1, concat_axis=2, tiled=True)]

    pad = pltpu.VMEM((blocks, frames, height, width + 2 * PAD, LANES), F32)
    piece = struct((frames, pixels // count, channels), BF16)
    cot_piece = struct((frames, height // count, width, channels), BF16)
    held = [temporal_kernel, w_expand, w_project]
    outs = call(
        functools.partial(spatial_fwd, count),
        [piece] * count + [cot_piece] * count + [struct(a.shape, a.dtype) for a in held],
        [
            pltpu.VMEM(clips.shape[1:], BF16),
            pltpu.VMEM(spatial_kernel.shape, F32),
            pad,
            pltpu.VMEM((frames, height, width, channels), F32),
            pltpu.SemaphoreType.DMA((2 + count + len(held),)),
        ],
        clips,
        cotangent,
        spatial_kernel,
        *held,
        far=3 + len(held),
    )
    firsts = to_columns(list(outs[:count]))
    cots = to_columns(list(outs[count : 2 * count]))
    temporal_kernel, w_expand, w_project = outs[2 * count :]

    column = (all_frames, columns, channels)
    back = struct((all_frames // count, columns, channels), BF16)
    outs = call(
        functools.partial(mlp_fwd, count, chunk),
        [
            struct(column, BF16),
            struct((tokens, channels), BF16),
            struct((tokens, hid), BF16),
            struct((tokens, channels), F32),
            struct((tokens, 1), F32),
        ],
        [
            pltpu.VMEM(column, F32),
            pltpu.VMEM(column, F32),
            pltpu.VMEM((tokens, hid), BF16),
        ],
        *firsts,
        temporal_kernel,
        norm_gain,
        w_expand,
        w_project,
    )
    branch, scaled, slope, normed, inv_std = outs

    sides = lax.axis_size("dp")
    staged = count == 4 and sides == 4
    half = (2 * count, hid // (sides * count), channels)
    outs = call(
        functools.partial(hidden_bwd, count, chunk, staged),
        [struct((tokens, hid), BF16)] + [struct(half, F32), struct(half, BF16)] * staged,
        [pltpu.VMEM((2 * half[0],) + half[1:], F32)] * staged + [pltpu.VMEM(column, F32)],
        *cots,
        slope,
        w_project,
        scaled,
    )
    d_pre = outs[0]
    shares = outs[1:]
    outs = call(
        functools.partial(token_bwd, count),
        [struct((2,) + back.shape, BF16)] * count,
        [pltpu.VMEM(column, F32), pltpu.VMEM(column, F32)],
        d_pre,
        normed,
        inv_std,
        temporal_kernel,
        norm_gain,
        w_expand,
        branch,
    )
    arrived = to_frames(list(outs))

    block_out, grad_clips = call(
        functools.partial(spatial_bwd, count),
        [struct(clips.shape, BF16)] * 2,
        [pad],
        *arrived,
        clips,
        cotangent,
        spatial_kernel,
    )
    if staged:
        grad_expand = scatter_grad(*shares, count, scale_factor, outs[0])
    else:
        whole = lax.dot_general(
            d_pre, scaled, (((0,), (0,)), ((), ())), preferred_element_type=F32
        )
        whole = lax.psum_scatter(whole, ("tm", "dp"), scatter_dimension=0, tiled=True)
        grad_expand = whole * scale_factor
    return (block_out, grad_clips, grad_expand)


def solution(mesh):
    in_specs = (
        P(("groups", "dp"), "tm", None, None, None),
        P(("groups", "dp"), "tm", None, None, None),
        P(),
        P(),
        P(),
        P(),
        P(),
    )
    out_specs = (
        P(("groups", "dp"), "tm", None, None, None),
        P(("groups", "dp"), "tm", None, None, None),
        P(("groups", "tm", "dp"), None),
    )
    return jax.shard_map(local, mesh=mesh, in_specs=in_specs, out_specs=out_specs, check_vma=False)
```

```python
import functools
import jax
import jax.numpy as jnp
from jax import lax
from jax.experimental import pallas as pl
from jax.experimental.pallas import tpu as pltpu
from jax.sharding import PartitionSpec as P

LANES = 128
PAD = 8
F32 = jnp.float32
BF16 = jnp.bfloat16
VMEM_LIMIT = 32 * 1024 * 1024


def call(body, outs, scratch, *args, cost=0, far=0, wait=(), limit=VMEM_LIMIT):
    specs = [pl.BlockSpec(memory_space=pltpu.HBM)] * far
    specs += [pl.BlockSpec(memory_space=pltpu.VMEM)] * (len(args) - far)
    args = [
        pltpu.with_memory_space_constraint(a, pltpu.HBM) if i < far else a
        for i, a in enumerate(args)
    ]
    given = len(args)
    for a in wait:
        specs.append(pl.BlockSpec(memory_space=pl.ANY))
        args.append(pltpu.with_memory_space_constraint(a, pltpu.HBM) if a.ndim == 5 else a)

    def kernel(*refs):
        body(*refs[:given], *refs[given + len(wait) :])

    return pl.pallas_call(
        kernel,
        out_shape=tuple(outs),
        in_specs=specs,
        out_specs=tuple([pl.BlockSpec(memory_space=pltpu.VMEM)] * len(outs)),
        scratch_shapes=list(scratch),
        cost_estimate=pl.CostEstimate(flops=cost, bytes_accessed=cost, transcendentals=0),
        compiler_params=pltpu.CompilerParams(vmem_limit_bytes=limit),
    )(*args)


def struct(shape, dtype):
    return jax.ShapeDtypeStruct(tuple(shape), dtype)


def slot_to(step, count):
    if count == 1:
        return 0
    return lax.rem(lax.axis_index("tm") + step, count)


def slot_from(step, count):
    if count == 1:
        return 0
    return lax.rem(lax.axis_index("tm") + count - step, count)


def partner(step, count):
    if count == 1:
        return 0
    return lax.bitwise_xor(lax.axis_index("tm"), step)


def swap(pieces):
    got = [pieces[0]]
    for step in range(1, len(pieces)):
        pairs = [(i, i ^ step) for i in range(len(pieces))]
        got.append(lax.ppermute(pieces[step], "tm", pairs))
    return got


def exchange(pieces):
    count = len(pieces)
    got = [pieces[0]]
    for step in range(1, count):
        pairs = [(i, (i + step) % count) for i in range(count)]
        got.append(lax.ppermute(pieces[step], "tm", pairs))
    return got


def conv_rows(pad_ref, kernel_ref, block, col, height, flip, emit):
    taps = kernel_ref.shape[0]
    lanes = slice(block * LANES, (block + 1) * LANES)
    radius = taps // 2
    acc = [None] * height
    for col_off in range(taps):
        shift = radius - col_off if flip else col_off - radius
        weights = [
            kernel_ref[row_off, pl.ds(col_off, 1), lanes] for row_off in range(taps)
        ]
        for row in range(height):
            values = pad_ref[block, :, row, pl.ds(PAD + col + shift, 8), :]
            for row_off in range(taps):
                out = row - radius + row_off if flip else row + radius - row_off
                if 0 <= out < height:
                    term = values * weights[row_off][None]
                    acc[out] = term if acc[out] is None else acc[out] + term
    for row in range(height):
        emit(row, acc[row])


def clear_pads(pad_ref, width):
    blocks, frames, height, _, lanes = pad_ref.shape
    zero = jnp.zeros((blocks, frames, height, PAD, lanes), F32)
    pad_ref[:, :, :, 0:PAD, :] = zero
    pad_ref[:, :, :, PAD + width : PAD + width + PAD, :] = zero


def spatial_fwd(count, *refs):
    clips_far, cot_far, kernel_far = refs[:3]
    held = (len(refs) - 3 - 2 * count - 5) // 2
    fars = refs[3 : 3 + held]
    refs = refs[3 + held :]
    firsts = refs[:count]
    cots = refs[count : 2 * count]
    nears = refs[2 * count : 2 * count + held]
    clips, kernel, pad_ref, flat, sems = refs[2 * count + held :]
    frames, height, width, channels = clips.shape
    blocks = channels // LANES
    pixels = height * width // count
    rows = height // count
    copies = [
        pltpu.make_async_copy(clips_far.at[0], clips, sems.at[0]),
        pltpu.make_async_copy(kernel_far, kernel, sems.at[1]),
    ]
    for step in range(count):
        base = slot_to(step, count) * rows
        copies.append(
            pltpu.make_async_copy(
                cot_far.at[0, :, pl.ds(base, rows)], cots[step], sems.at[2 + step]
            )
        )
    for index in range(held):
        copies.append(
            pltpu.make_async_copy(fars[index], nears[index], sems.at[2 + count + index])
        )
    for copy in copies:
        copy.start()
    clear_pads(pad_ref, width)
    copies[0].wait()
    for block in range(blocks):
        lanes = slice(block * LANES, (block + 1) * LANES)
        pad_ref[block, :, :, PAD : PAD + width, :] = clips[:, :, :, lanes].astype(F32)
    copies[1].wait()
    for block in range(blocks):
        lanes = slice(block * LANES, (block + 1) * LANES)
        for col in range(0, width, 8):

            def emit(row, value):
                flat[:, row, pl.ds(col, 8), lanes] = value

            conv_rows(pad_ref, kernel, block, col, height, False, emit)
    for step in range(count):
        base = slot_to(step, count) * rows
        firsts[step][...] = (
            flat[:, pl.ds(base, rows), :, :].reshape(frames, pixels, channels).astype(BF16)
        )
    for copy in copies[2:]:
        copy.wait()


def spatial_bwd(count, *refs):
    pieces = refs[:count]
    clips, cot, kernel, block_out, out_ref, pad_ref = refs[count:]
    _, frames, height, width, channels = cot.shape
    blocks = channels // LANES
    rows = height // count
    clear_pads(pad_ref, width)
    for step in range(count):
        base = partner(step, count) * rows
        for block in range(blocks):
            lanes = slice(block * LANES, (block + 1) * LANES)
            piece = pieces[step][1, :, :, lanes].astype(F32).reshape(frames, rows, width, LANES)
            pad_ref[block, :, pl.ds(base, rows), PAD : PAD + width, :] = piece
        here = (0, slice(None), pl.ds(base, rows))
        branch = pieces[step][0].reshape(frames, rows, width, channels).astype(F32)
        block_out[here] = (clips[here].astype(F32) + branch).astype(BF16)
    for block in range(blocks):
        lanes = slice(block * LANES, (block + 1) * LANES)
        for col in range(0, width, 16):
            halves = []
            for part in range(2):
                rows_out = []
                conv_rows(
                    pad_ref, kernel, block, col + 8 * part, height, True,
                    lambda row, value: rows_out.append(value),
                )
                halves.append(rows_out)
            for row in range(height):
                total = jnp.concatenate([halves[0][row], halves[1][row]], axis=1)
                total = total + cot[0, :, row, pl.ds(col, 16), lanes].astype(F32)
                out_ref[0, :, row, pl.ds(col, 16), lanes] = total.astype(BF16)


def mix_frames(source, target, kernel, flip):
    frames = source.shape[0]
    taps = kernel.shape[0]
    radius = taps // 2
    if frames <= 16:
        for out in range(frames):
            total = None
            for inp in range(frames):
                lag = (out - inp if flip else inp - out) + radius
                if 0 <= lag < taps:
                    term = kernel[pl.ds(lag, 1), :] * source[inp]
                    total = term if total is None else total + term
            target[out] = total.astype(BF16).astype(F32)
        return

    def one(out, carry):
        def tap(inp, total):
            lag = (out - inp if flip else inp - out) + radius
            return total + kernel[pl.ds(lag, 1), :] * source[inp]

        low = jnp.maximum(out - radius, 0)
        high = jnp.minimum(out + radius + 1, frames)
        total = lax.fori_loop(low, high, tap, jnp.zeros(source.shape[1:], F32))
        target[out] = total.astype(BF16).astype(F32)
        return carry

    lax.fori_loop(0, frames, one, 0)


def place_frames(count, pieces, target):
    for step in range(count):
        frames = pieces[step].shape[0]
        base = slot_from(step, count) * frames
        piece = pieces[step][...].reshape((frames,) + target.shape[1:])
        target[pl.ds(base, frames)] = piece.astype(target.dtype)


def mlp_fwd(count, chunk, *refs):
    pieces = refs[:count]
    taps, gain, w_expand, w_project = refs[count : count + 4]
    branch, scaled, slope, normed, inv_std, mixed_in, mixed, hidden = refs[count + 4 :]
    frames, pixels, channels = mixed_in.shape
    tokens = frames * pixels
    place_frames(count, pieces, mixed_in)
    mix_frames(mixed_in, mixed, taps, False)
    values = mixed[...].reshape(tokens, channels)
    average = jnp.mean(values, axis=-1, keepdims=True)
    centred = values - average
    inverse = lax.rsqrt(jnp.mean(centred * centred, axis=-1, keepdims=True) + 1e-06)
    inv_std[...] = inverse
    norm = centred * inverse
    normed[...] = norm
    scaled[...] = (norm * gain[...].reshape(1, channels)).astype(BF16)
    for start in range(0, w_expand.shape[1], chunk):
        part = slice(start, start + chunk)
        pre = jnp.dot(scaled[...], w_expand[:, part], preferred_element_type=F32)
        cdf = 0.5 + 0.5 * lax.erf(pre * 0.7071067811865476)
        hidden[:, part] = (pre * cdf).astype(BF16)
        slope[:, part] = (cdf + pre * jnp.exp(-0.5 * pre * pre) * 0.3989422804014327).astype(BF16)
    out = jnp.dot(hidden[...], w_project[...], preferred_element_type=F32).astype(BF16)
    branch[...] = out.reshape(branch.shape)


def hidden_bwd(count, steps, with_grad, final, *refs):
    pieces = refs[: len(steps)]
    slope, w_project, scaled = refs[len(steps) : len(steps) + 3]
    refs = refs[len(steps) + 3 :]
    channels = scaled.shape[1]
    rows = scaled.shape[0] // count
    sources = [pl.multiple_of(slot_from(step, count) * rows, rows) for step in steps]
    grads = jnp.concatenate([p[...].reshape(rows, channels) for p in pieces], axis=0)
    d_hidden = lax.dot_general(
        grads, w_project[...], (((1,), (1,)), ((), ())), preferred_element_type=F32
    )
    steep = jnp.concatenate([slope[pl.ds(source, rows), :] for source in sources], axis=0)
    result = (d_hidden * steep.astype(F32)).astype(BF16)
    if not with_grad:
        refs[-1][...] = result
        return
    inputs = jnp.concatenate([scaled[pl.ds(source, rows), :] for source in sources], axis=0)
    share = lax.dot_general(result, inputs, (((0,), (0,)), ((), ())), preferred_element_type=F32)
    if not final:
        d_pre, full = refs
        d_pre[...] = result
        full[...] = share.reshape(full.shape)
        return
    before, d_pre, keep, send, full = refs
    d_pre[...] = result
    full[...] = share.reshape(full.shape)
    core = lax.rem(lax.axis_index("dp"), 2)
    for pair in range(full.shape[0] // 2):
        mine, other = 2 * pair + core, 2 * pair + 1 - core
        keep[pair] = full[mine] + before[mine]
        send[pair] = (full[other] + before[other]).astype(BF16)


def token_bwd(count, groups, *refs):
    parts, refs = refs[: len(groups)], refs[len(groups) :]
    normed, inv_std, taps, gain, w_expand, branch = refs[:6]
    outs = refs[6 : count + 6]
    d_second, d_first = refs[count + 6 :]
    frames, pixels, channels = d_second.shape
    own = frames // count
    last = (((1,), (1,)), ((), ()))
    for steps, d_pre in zip(groups, parts):
        d_scaled = lax.dot_general(d_pre[...], w_expand[...], last, preferred_element_type=F32)
        d_scaled = d_scaled.reshape(len(steps), own, pixels, channels)
        for index, step in enumerate(steps):
            d_second[pl.ds(slot_from(step, count) * own, own)] = d_scaled[index]
    d_normed = d_second[...].reshape(frames * pixels, channels) * gain[...].reshape(1, channels)
    norm = normed[...]
    d_tokens = inv_std[...] * (
        d_normed
        - jnp.mean(d_normed, axis=-1, keepdims=True)
        - norm * jnp.mean(d_normed * norm, axis=-1, keepdims=True)
    )
    d_second[...] = d_tokens.astype(BF16).astype(F32).reshape(frames, pixels, channels)
    mix_frames(d_second, d_first, taps, True)
    for step in range(count):
        base = partner(step, count) * own
        outs[step][0] = branch[pl.ds(base, own)]
        outs[step][1] = d_first[pl.ds(base, own)].astype(BF16)


def fold_pair(keep_in, got, keep, send):
    side = lax.div(lax.axis_index("dp"), 2)
    for slot in range(keep.shape[0]):
        mine, other = 2 * slot + side, 2 * slot + 1 - side
        keep[slot] = keep_in[mine] + got[mine].astype(F32)
        send[slot] = (keep_in[other] + got[other].astype(F32)).astype(BF16)


def fold_near(keep_in, got, keep, *sends):
    me = lax.axis_index("tm")
    for far in range(2):
        mine = lax.bitwise_xor(me, 2 * far)
        other = lax.bitwise_xor(me, 2 * far + 1)
        keep[far] = keep_in[mine] + got[mine].astype(F32)
        sends[far][...] = (keep_in[other] + got[other].astype(F32)).astype(BF16)


def fold_far(keep_in, got, got_far, keep, send):
    keep[...] = keep_in[0] + got[...].astype(F32)
    send[...] = (keep_in[1] + got_far[...].astype(F32)).astype(BF16)


def fold_last(scale_factor, keep_in, *refs):
    total = keep_in[...]
    for got in refs[:-1]:
        total = total + got[...].astype(F32)
    refs[-1][...] = total * scale_factor


def scatter_grad(keep, send, count, scale_factor, d_first):
    channels = keep.shape[-1]
    block = keep.shape[1]
    quarter = (count, block, channels)
    piece = (block, channels)
    got = lax.ppermute(send, "dp", [(i, i ^ 1) for i in range(4)])
    keep, send = call(
        fold_pair, [struct(quarter, F32), struct(quarter, BF16)], [], keep, got, wait=[d_first]
    )
    got = lax.ppermute(send, "dp", [(i, i ^ 2) for i in range(4)])
    pair = (2,) + piece
    keep, *sends = call(
        fold_near, [struct(pair, F32), struct(piece, BF16), struct(piece, BF16)], [], keep, got
    )
    near = [lax.ppermute(send, "tm", [(i, i ^ 1) for i in range(4)]) for send in sends]
    keep, send = call(
        fold_far, [struct(piece, F32), struct(piece, BF16)], [], keep, *near
    )
    got = lax.ppermute(send, "tm", [(i, i ^ 2) for i in range(4)])
    return call(functools.partial(fold_last, scale_factor), [struct(piece, F32)], [], keep, got)[0]


def local(clips, cotangent, spatial_kernel, temporal_kernel, norm_gain, w_expand, w_project):
    _, frames, height, width, channels = clips.shape
    members = lax.axis_size("tm")
    device_count = members * lax.axis_size("dp")
    pixels = height * width
    scale_factor = float(clips.shape[0] * frames * pixels * device_count) ** (-0.5)
    hid = w_expand.shape[1]
    chunk = 256
    blocks = channels // LANES
    count = members if members in (2, 4, 8) and height % members == 0 else 1
    all_frames = frames * members
    columns = pixels // members
    tokens = all_frames * columns

    def to_columns(pieces):
        if count > 1:
            return exchange(pieces)
        whole = pieces[0].reshape(1, frames, pixels, channels)
        return [lax.all_to_all(whole, "tm", split_axis=2, concat_axis=1, tiled=True)[0]]

    def to_frames(pieces):
        if count > 1:
            return swap(pieces)
        return [lax.all_to_all(pieces[0], "tm", split_axis=1, concat_axis=2, tiled=True)]

    pad = pltpu.VMEM((blocks, frames, height, width + 2 * PAD, LANES), F32)
    piece = struct((frames, pixels // count, channels), BF16)
    cot_piece = struct((frames, height // count, width, channels), BF16)
    held = [temporal_kernel, w_expand, w_project]
    outs = call(
        functools.partial(spatial_fwd, count),
        [piece] * count + [cot_piece] * count + [struct(a.shape, a.dtype) for a in held],
        [
            pltpu.VMEM(clips.shape[1:], BF16),
            pltpu.VMEM(spatial_kernel.shape, F32),
            pad,
            pltpu.VMEM((frames, height, width, channels), F32),
            pltpu.SemaphoreType.DMA((2 + count + len(held),)),
        ],
        clips,
        cotangent,
        spatial_kernel,
        *held,
        far=3 + len(held),
    )
    firsts = to_columns(list(outs[:count]))
    cots = to_columns(list(outs[count : 2 * count]))
    temporal_kernel, w_expand, w_project = outs[2 * count :]

    column = (all_frames, columns, channels)
    back = struct((all_frames // count, columns, channels), BF16)
    outs = call(
        functools.partial(mlp_fwd, count, chunk),
        [
            struct(column, BF16),
            struct((tokens, channels), BF16),
            struct((tokens, hid), BF16),
            struct((tokens, channels), F32),
            struct((tokens, 1), F32),
        ],
        [
            pltpu.VMEM(column, F32),
            pltpu.VMEM(column, F32),
            pltpu.VMEM((tokens, hid), BF16),
        ],
        *firsts,
        temporal_kernel,
        norm_gain,
        w_expand,
        w_project,
    )
    branch, scaled, slope, normed, inv_std = outs

    sides = lax.axis_size("dp")
    staged = count == 4 and sides == 4
    half = (2 * count, hid // (sides * count), channels)
    whole = (2 * half[0],) + half[1:]
    groups = [[0, 1], [2, 3]] if staged else [list(range(count))]
    parts, shares = [], []
    for steps in groups:
        rows = len(steps) * tokens // count
        final = steps is groups[-1]
        results = [struct((rows, hid), BF16)]
        if staged and final:
            results += [struct(half, F32), struct(half, BF16)]
        elif staged:
            results += [struct(whole, F32)]
        part, *shares = call(
            functools.partial(hidden_bwd, count, steps, staged, final),
            results,
            [pltpu.VMEM(whole, F32)] if staged and final else [],
            *[cots[step] for step in steps],
            slope,
            w_project,
            scaled,
            *shares,
        )
        parts.append(part)
    outs = call(
        functools.partial(token_bwd, count, groups),
        [struct((2,) + back.shape, BF16)] * count,
        [pltpu.VMEM(column, F32), pltpu.VMEM(column, F32)],
        *parts,
        normed,
        inv_std,
        temporal_kernel,
        norm_gain,
        w_expand,
        branch,
    )
    arrived = to_frames(list(outs))

    block_out, grad_clips = call(
        functools.partial(spatial_bwd, count),
        [struct(clips.shape, BF16)] * 2,
        [pad],
        *arrived,
        clips,
        cotangent,
        spatial_kernel,
    )
    if staged:
        grad_expand = scatter_grad(*shares, count, scale_factor, outs[0])
    else:
        whole = lax.dot_general(
            parts[0], scaled, (((0,), (0,)), ((), ())), preferred_element_type=F32
        )
        whole = lax.psum_scatter(whole, ("tm", "dp"), scatter_dimension=0, tiled=True)
        grad_expand = whole * scale_factor
    return (block_out, grad_clips, grad_expand)


def solution(mesh):
    in_specs = (
        P(("groups", "dp"), "tm", None, None, None),
        P(("groups", "dp"), "tm", None, None, None),
        P(),
        P(),
        P(),
        P(),
        P(),
    )
    out_specs = (
        P(("groups", "dp"), "tm", None, None, None),
        P(("groups", "dp"), "tm", None, None, None),
        P(("groups", "tm", "dp"), None),
    )
    return jax.shard_map(local, mesh=mesh, in_specs=in_specs, out_specs=out_specs, check_vma=False)
```

```python
import functools
import jax
import jax.numpy as jnp
from jax import lax
from jax.experimental import pallas as pl
from jax.experimental.pallas import tpu as pltpu
from jax.sharding import PartitionSpec as P

LANES = 128
PAD = 8
F32 = jnp.float32
BF16 = jnp.bfloat16
VMEM_LIMIT = 32 * 1024 * 1024


def call(body, outs, scratch, *args, cost=0, far=0, wait=(), limit=VMEM_LIMIT):
    specs = [pl.BlockSpec(memory_space=pltpu.HBM)] * far
    specs += [pl.BlockSpec(memory_space=pltpu.VMEM)] * (len(args) - far)
    args = [
        pltpu.with_memory_space_constraint(a, pltpu.HBM) if i < far else a
        for i, a in enumerate(args)
    ]
    given = len(args)
    for a in wait:
        specs.append(pl.BlockSpec(memory_space=pl.ANY))
        args.append(pltpu.with_memory_space_constraint(a, pltpu.HBM) if a.ndim == 5 else a)

    def kernel(*refs):
        body(*refs[:given], *refs[given + len(wait) :])

    return pl.pallas_call(
        kernel,
        out_shape=tuple(outs),
        in_specs=specs,
        out_specs=tuple([pl.BlockSpec(memory_space=pltpu.VMEM)] * len(outs)),
        scratch_shapes=list(scratch),
        cost_estimate=pl.CostEstimate(flops=cost, bytes_accessed=cost, transcendentals=0),
        compiler_params=pltpu.CompilerParams(vmem_limit_bytes=limit),
    )(*args)


def struct(shape, dtype):
    return jax.ShapeDtypeStruct(tuple(shape), dtype)


def slot_to(step, count):
    if count == 1:
        return 0
    return lax.rem(lax.axis_index("tm") + step, count)


def slot_from(step, count):
    if count == 1:
        return 0
    return lax.rem(lax.axis_index("tm") + count - step, count)


def partner(step, count):
    if count == 1:
        return 0
    return lax.bitwise_xor(lax.axis_index("tm"), step)


def swap(pieces):
    got = [pieces[0]]
    for step in range(1, len(pieces)):
        pairs = [(i, i ^ step) for i in range(len(pieces))]
        got.append(lax.ppermute(pieces[step], "tm", pairs))
    return got


def exchange(pieces):
    count = len(pieces)
    got = [pieces[0]]
    for step in range(1, count):
        pairs = [(i, (i + step) % count) for i in range(count)]
        got.append(lax.ppermute(pieces[step], "tm", pairs))
    return got


def conv_rows(pad_ref, kernel_ref, block, col, height, flip, emit, low=0, high=None):
    taps = kernel_ref.shape[0]
    lanes = slice(block * LANES, (block + 1) * LANES)
    radius = taps // 2
    high = height if high is None else high
    acc = [None] * height
    for col_off in range(taps):
        shift = radius - col_off if flip else col_off - radius
        weights = [
            kernel_ref[row_off, pl.ds(col_off, 1), lanes] for row_off in range(taps)
        ]
        for row in range(max(low - radius, 0), min(high + radius, height)):
            values = pad_ref[block, :, row, pl.ds(PAD + col + shift, 8), :]
            for row_off in range(taps):
                out = row - radius + row_off if flip else row + radius - row_off
                if low <= out < high:
                    term = values * weights[row_off][None]
                    acc[out] = term if acc[out] is None else acc[out] + term
    for row in range(low, high):
        emit(row, acc[row])


def clear_pads(pad_ref, width):
    blocks, frames, height, _, lanes = pad_ref.shape
    zero = jnp.zeros((blocks, frames, height, PAD, lanes), F32)
    pad_ref[:, :, :, 0:PAD, :] = zero
    pad_ref[:, :, :, PAD + width : PAD + width + PAD, :] = zero


def spatial_fwd(count, *refs):
    clips_far, cot_far, kernel_far = refs[:3]
    held = (len(refs) - 3 - 2 * count - 5) // 2
    fars = refs[3 : 3 + held]
    refs = refs[3 + held :]
    firsts = refs[:count]
    cots = refs[count : 2 * count]
    nears = refs[2 * count : 2 * count + held]
    clips, kernel, pad_ref, flat, sems = refs[2 * count + held :]
    frames, height, width, channels = clips.shape
    blocks = channels // LANES
    pixels = height * width // count
    rows = height // count
    copies = [
        pltpu.make_async_copy(clips_far.at[0], clips, sems.at[0]),
        pltpu.make_async_copy(kernel_far, kernel, sems.at[1]),
    ]
    for step in range(count):
        base = slot_to(step, count) * rows
        copies.append(
            pltpu.make_async_copy(
                cot_far.at[0, :, pl.ds(base, rows)], cots[step], sems.at[2 + step]
            )
        )
    for index in range(held):
        copies.append(
            pltpu.make_async_copy(fars[index], nears[index], sems.at[2 + count + index])
        )
    for copy in copies:
        copy.start()
    clear_pads(pad_ref, width)
    copies[0].wait()
    for block in range(blocks):
        lanes = slice(block * LANES, (block + 1) * LANES)
        pad_ref[block, :, :, PAD : PAD + width, :] = clips[:, :, :, lanes].astype(F32)
    copies[1].wait()
    for block in range(blocks):
        lanes = slice(block * LANES, (block + 1) * LANES)
        for col in range(0, width, 8):

            def emit(row, value):
                flat[:, row, pl.ds(col, 8), lanes] = value

            conv_rows(pad_ref, kernel, block, col, height, False, emit)
    for step in range(count):
        base = partner(step, count) * rows
        firsts[step][...] = (
            flat[:, pl.ds(base, rows), :, :].reshape(frames, pixels, channels).astype(BF16)
        )
    for copy in copies[2:]:
        copy.wait()


def half_rows(pad_ref, kernel, flat, half):
    blocks, _, height, padded, _ = pad_ref.shape
    for value in range(2):
        low = value * height // 2

        @pl.when(half == value)
        def _():
            for block in range(blocks):
                lanes = slice(block * LANES, (block + 1) * LANES)
                for col in range(0, padded - 2 * PAD, 8):

                    def emit(row, result):
                        flat[:, row - low, pl.ds(col, 8), lanes] = result

                    conv_rows(
                        pad_ref, kernel, block, col, height, False, emit, low, low + height // 2
                    )


def spatial_far(clips_far, kernel_far, first_a, first_b, pad_ref, kernel, clips, flat, sems):
    frames, height, width, channels = clips.shape
    copies = [
        pltpu.make_async_copy(clips_far.at[0], clips, sems.at[0]),
        pltpu.make_async_copy(kernel_far, kernel, sems.at[1]),
    ]
    for copy in copies:
        copy.start()
    clear_pads(pad_ref, width)
    copies[0].wait()
    for block in range(channels // LANES):
        lanes = slice(block * LANES, (block + 1) * LANES)
        pad_ref[block, :, :, PAD : PAD + width, :] = clips[:, :, :, lanes].astype(F32)
    copies[1].wait()
    half = 1 - lax.div(lax.axis_index("tm"), 2)
    half_rows(pad_ref, kernel, flat, half)
    rows = height // 4
    for step, out in ((2, first_a), (3, first_b)):
        base = partner(step, 4) * rows - half * (height // 2)
        out[...] = flat[:, pl.ds(base, rows)].reshape(out.shape).astype(BF16)


def spatial_near(held, *refs):
    cot_far, fars = refs[0], refs[1 : 1 + held]
    pad_ref, kernel, first_own, first_near = refs[1 + held : 5 + held]
    cots, nears = refs[5 + held : 9 + held], refs[9 + held : 9 + 2 * held]
    flat, sems = refs[9 + 2 * held :]
    height = pad_ref.shape[2]
    rows = height // 4
    copies = []
    for step in range(4):
        base = slot_to(step, 4) * rows
        copies.append(
            pltpu.make_async_copy(cot_far.at[0, :, pl.ds(base, rows)], cots[step], sems.at[step])
        )
    for index in range(held):
        copies.append(pltpu.make_async_copy(fars[index], nears[index], sems.at[4 + index]))
    for copy in copies:
        copy.start()
    half = lax.div(lax.axis_index("tm"), 2)
    half_rows(pad_ref, kernel, flat, half)
    for step, out in ((0, first_own), (1, first_near)):
        base = partner(step, 4) * rows - half * (height // 2)
        out[...] = flat[:, pl.ds(base, rows)].reshape(out.shape).astype(BF16)
    for copy in copies:
        copy.wait()


def spatial_bwd(count, *refs):
    pieces = refs[:count]
    clips, cot, kernel, block_out, out_ref, pad_ref = refs[count:]
    _, frames, height, width, channels = cot.shape
    blocks = channels // LANES
    rows = height // count
    clear_pads(pad_ref, width)
    for step in range(count):
        base = partner(step, count) * rows
        for block in range(blocks):
            lanes = slice(block * LANES, (block + 1) * LANES)
            piece = pieces[step][1, :, :, lanes].astype(F32).reshape(frames, rows, width, LANES)
            pad_ref[block, :, pl.ds(base, rows), PAD : PAD + width, :] = piece
        here = (0, slice(None), pl.ds(base, rows))
        branch = pieces[step][0].reshape(frames, rows, width, channels).astype(F32)
        block_out[here] = (clips[here].astype(F32) + branch).astype(BF16)
    for block in range(blocks):
        lanes = slice(block * LANES, (block + 1) * LANES)
        for col in range(0, width, 16):
            halves = []
            for part in range(2):
                rows_out = []
                conv_rows(
                    pad_ref, kernel, block, col + 8 * part, height, True,
                    lambda row, value: rows_out.append(value),
                )
                halves.append(rows_out)
            for row in range(height):
                total = jnp.concatenate([halves[0][row], halves[1][row]], axis=1)
                total = total + cot[0, :, row, pl.ds(col, 16), lanes].astype(F32)
                out_ref[0, :, row, pl.ds(col, 16), lanes] = total.astype(BF16)


def mix_frames(source, target, kernel, flip):
    frames = source.shape[0]
    taps = kernel.shape[0]
    radius = taps // 2
    if frames <= 16:
        for out in range(frames):
            total = None
            for inp in range(frames):
                lag = (out - inp if flip else inp - out) + radius
                if 0 <= lag < taps:
                    term = kernel[pl.ds(lag, 1), :] * source[inp]
                    total = term if total is None else total + term
            target[out] = total.astype(BF16).astype(F32)
        return

    def one(out, carry):
        def tap(inp, total):
            lag = (out - inp if flip else inp - out) + radius
            return total + kernel[pl.ds(lag, 1), :] * source[inp]

        low = jnp.maximum(out - radius, 0)
        high = jnp.minimum(out + radius + 1, frames)
        total = lax.fori_loop(low, high, tap, jnp.zeros(source.shape[1:], F32))
        target[out] = total.astype(BF16).astype(F32)
        return carry

    lax.fori_loop(0, frames, one, 0)


def place_frames(count, pieces, target):
    for step in range(count):
        frames = pieces[step].shape[0]
        base = partner(step, count) * frames
        piece = pieces[step][...].reshape((frames,) + target.shape[1:])
        target[pl.ds(base, frames)] = piece.astype(target.dtype)


def mlp_fwd(count, chunk, *refs):
    pieces = refs[:count]
    taps, gain, w_expand, w_project = refs[count : count + 4]
    branch, scaled, slope, normed, inv_std, mixed_in, mixed, hidden = refs[count + 4 :]
    frames, pixels, channels = mixed_in.shape
    tokens = frames * pixels
    place_frames(count, pieces, mixed_in)
    mix_frames(mixed_in, mixed, taps, False)
    values = mixed[...].reshape(tokens, channels)
    average = jnp.mean(values, axis=-1, keepdims=True)
    centred = values - average
    inverse = lax.rsqrt(jnp.mean(centred * centred, axis=-1, keepdims=True) + 1e-06)
    inv_std[...] = inverse
    norm = centred * inverse
    normed[...] = norm
    scaled[...] = (norm * gain[...].reshape(1, channels)).astype(BF16)
    for start in range(0, w_expand.shape[1], chunk):
        part = slice(start, start + chunk)
        pre = jnp.dot(scaled[...], w_expand[:, part], preferred_element_type=F32)
        cdf = 0.5 + 0.5 * lax.erf(pre * 0.7071067811865476)
        hidden[:, part] = (pre * cdf).astype(BF16)
        slope[:, part] = (cdf + pre * jnp.exp(-0.5 * pre * pre) * 0.3989422804014327).astype(BF16)
    out = jnp.dot(hidden[...], w_project[...], preferred_element_type=F32).astype(BF16)
    branch[...] = out.reshape(branch.shape)


def hidden_bwd(count, steps, with_grad, final, *refs):
    pieces = refs[: len(steps)]
    slope, w_project, scaled = refs[len(steps) : len(steps) + 3]
    refs = refs[len(steps) + 3 :]
    channels = scaled.shape[1]
    rows = scaled.shape[0] // count
    sources = [pl.multiple_of(slot_from(step, count) * rows, rows) for step in steps]
    grads = jnp.concatenate([p[...].reshape(rows, channels) for p in pieces], axis=0)
    d_hidden = lax.dot_general(
        grads, w_project[...], (((1,), (1,)), ((), ())), preferred_element_type=F32
    )
    steep = jnp.concatenate([slope[pl.ds(source, rows), :] for source in sources], axis=0)
    result = (d_hidden * steep.astype(F32)).astype(BF16)
    if not with_grad:
        refs[-1][...] = result
        return
    inputs = jnp.concatenate([scaled[pl.ds(source, rows), :] for source in sources], axis=0)
    share = lax.dot_general(result, inputs, (((0,), (0,)), ((), ())), preferred_element_type=F32)
    if not final:
        d_pre, full = refs
        d_pre[...] = result
        full[...] = share.reshape(full.shape)
        return
    before, d_pre, keep, send, full = refs
    d_pre[...] = result
    full[...] = share.reshape(full.shape)
    core = lax.rem(lax.axis_index("dp"), 2)
    for pair in range(full.shape[0] // 2):
        mine, other = 2 * pair + core, 2 * pair + 1 - core
        keep[pair] = full[mine] + before[mine]
        send[pair] = (full[other] + before[other]).astype(BF16)


def token_bwd(count, groups, *refs):
    parts, refs = refs[: len(groups)], refs[len(groups) :]
    normed, inv_std, taps, gain, w_expand, branch = refs[:6]
    outs = refs[6 : count + 6]
    d_second, d_first = refs[count + 6 :]
    frames, pixels, channels = d_second.shape
    own = frames // count
    last = (((1,), (1,)), ((), ()))
    for steps, d_pre in zip(groups, parts):
        d_scaled = lax.dot_general(d_pre[...], w_expand[...], last, preferred_element_type=F32)
        d_scaled = d_scaled.reshape(len(steps), own, pixels, channels)
        for index, step in enumerate(steps):
            d_second[pl.ds(slot_from(step, count) * own, own)] = d_scaled[index]
    d_normed = d_second[...].reshape(frames * pixels, channels) * gain[...].reshape(1, channels)
    norm = normed[...]
    d_tokens = inv_std[...] * (
        d_normed
        - jnp.mean(d_normed, axis=-1, keepdims=True)
        - norm * jnp.mean(d_normed * norm, axis=-1, keepdims=True)
    )
    d_second[...] = d_tokens.astype(BF16).astype(F32).reshape(frames, pixels, channels)
    mix_frames(d_second, d_first, taps, True)
    for step in range(count):
        base = partner(step, count) * own
        outs[step][0] = branch[pl.ds(base, own)]
        outs[step][1] = d_first[pl.ds(base, own)].astype(BF16)


def fold_pair(keep_in, got, keep, send):
    side = lax.div(lax.axis_index("dp"), 2)
    for slot in range(keep.shape[0]):
        mine, other = 2 * slot + side, 2 * slot + 1 - side
        keep[slot] = keep_in[mine] + got[mine].astype(F32)
        send[slot] = (keep_in[other] + got[other].astype(F32)).astype(BF16)


def fold_near(keep_in, got, keep, *sends):
    me = lax.axis_index("tm")
    for far in range(2):
        mine = lax.bitwise_xor(me, 2 * far)
        other = lax.bitwise_xor(me, 2 * far + 1)
        keep[far] = keep_in[mine] + got[mine].astype(F32)
        sends[far][...] = (keep_in[other] + got[other].astype(F32)).astype(BF16)


def fold_far(keep_in, got, got_far, keep, send):
    keep[...] = keep_in[0] + got[...].astype(F32)
    send[...] = (keep_in[1] + got_far[...].astype(F32)).astype(BF16)


def fold_last(scale_factor, keep_in, *refs):
    total = keep_in[...]
    for got in refs[:-1]:
        total = total + got[...].astype(F32)
    refs[-1][...] = total * scale_factor


def scatter_grad(keep, send, count, scale_factor, d_first):
    channels = keep.shape[-1]
    block = keep.shape[1]
    quarter = (count, block, channels)
    piece = (block, channels)
    got = lax.ppermute(send, "dp", [(i, i ^ 1) for i in range(4)])
    keep, send = call(
        fold_pair, [struct(quarter, F32), struct(quarter, BF16)], [], keep, got, wait=[d_first]
    )
    got = lax.ppermute(send, "dp", [(i, i ^ 2) for i in range(4)])
    pair = (2,) + piece
    keep, *sends = call(
        fold_near, [struct(pair, F32), struct(piece, BF16), struct(piece, BF16)], [], keep, got
    )
    near = [lax.ppermute(send, "tm", [(i, i ^ 1) for i in range(4)]) for send in sends]
    keep, send = call(
        fold_far, [struct(piece, F32), struct(piece, BF16)], [], keep, *near
    )
    got = lax.ppermute(send, "tm", [(i, i ^ 2) for i in range(4)])
    return call(functools.partial(fold_last, scale_factor), [struct(piece, F32)], [], keep, got)[0]


def local(clips, cotangent, spatial_kernel, temporal_kernel, norm_gain, w_expand, w_project):
    _, frames, height, width, channels = clips.shape
    members = lax.axis_size("tm")
    device_count = members * lax.axis_size("dp")
    pixels = height * width
    scale_factor = float(clips.shape[0] * frames * pixels * device_count) ** (-0.5)
    hid = w_expand.shape[1]
    chunk = 256
    blocks = channels // LANES
    count = members if members in (2, 4, 8) and height % members == 0 else 1
    all_frames = frames * members
    columns = pixels // members
    tokens = all_frames * columns

    def to_columns(pieces):
        if count > 1:
            return exchange(pieces)
        whole = pieces[0].reshape(1, frames, pixels, channels)
        return [lax.all_to_all(whole, "tm", split_axis=2, concat_axis=1, tiled=True)[0]]

    def to_frames(pieces):
        if count > 1:
            return swap(pieces)
        return [lax.all_to_all(pieces[0], "tm", split_axis=1, concat_axis=2, tiled=True)]

    pad = pltpu.VMEM((blocks, frames, height, width + 2 * PAD, LANES), F32)
    piece = struct((frames, pixels // count, channels), BF16)
    cot_piece = struct((frames, height // count, width, channels), BF16)
    held = [temporal_kernel, w_expand, w_project]
    kept = [struct(a.shape, a.dtype) for a in held]
    image = (frames, height, width, channels)
    if count == 4:
        half_image = pltpu.VMEM((frames, height // 2, width, channels), F32)
        *far, padded, taps = call(
            spatial_far,
            [piece] * 2 + [struct(pad.shape, F32), struct(spatial_kernel.shape, F32)],
            [pltpu.VMEM(image, BF16), half_image, pltpu.SemaphoreType.DMA((2,))],
            clips,
            spatial_kernel,
            far=2,
        )
        outs = call(
            functools.partial(spatial_near, len(held)),
            [piece] * 2 + [cot_piece] * count + kept,
            [half_image, pltpu.SemaphoreType.DMA((count + len(held),))],
            cotangent,
            *held,
            padded,
            taps,
            far=1 + len(held),
        )
        outs = [outs[0], outs[1], *far, *outs[2:]]
    else:
        outs = call(
            functools.partial(spatial_fwd, count),
            [piece] * count + [cot_piece] * count + [struct(a.shape, a.dtype) for a in held],
            [
                pltpu.VMEM(clips.shape[1:], BF16),
                pltpu.VMEM(spatial_kernel.shape, F32),
                pad,
                pltpu.VMEM((frames, height, width, channels), F32),
                pltpu.SemaphoreType.DMA((2 + count + len(held),)),
            ],
            clips,
            cotangent,
            spatial_kernel,
            *held,
            far=3 + len(held),
        )
    firsts = swap(outs[:count]) if count > 1 else to_columns(list(outs[:count]))
    cots = to_columns(list(outs[count : 2 * count]))
    temporal_kernel, w_expand, w_project = outs[2 * count :]

    column = (all_frames, columns, channels)
    back = struct((all_frames // count, columns, channels), BF16)
    outs = call(
        functools.partial(mlp_fwd, count, chunk),
        [
            struct(column, BF16),
            struct((tokens, channels), BF16),
            struct((tokens, hid), BF16),
            struct((tokens, channels), F32),
            struct((tokens, 1), F32),
        ],
        [
            pltpu.VMEM(column, F32),
            pltpu.VMEM(column, F32),
            pltpu.VMEM((tokens, hid), BF16),
        ],
        *firsts,
        temporal_kernel,
        norm_gain,
        w_expand,
        w_project,
    )
    branch, scaled, slope, normed, inv_std = outs

    sides = lax.axis_size("dp")
    staged = count == 4 and sides == 4
    half = (2 * count, hid // (sides * count), channels)
    whole = (2 * half[0],) + half[1:]
    groups = [[0, 1], [2, 3]] if staged else [list(range(count))]
    parts, shares = [], []
    for steps in groups:
        rows = len(steps) * tokens // count
        final = steps is groups[-1]
        results = [struct((rows, hid), BF16)]
        if staged and final:
            results += [struct(half, F32), struct(half, BF16)]
        elif staged:
            results += [struct(whole, F32)]
        part, *shares = call(
            functools.partial(hidden_bwd, count, steps, staged, final),
            results,
            [pltpu.VMEM(whole, F32)] if staged and final else [],
            *[cots[step] for step in steps],
            slope,
            w_project,
            scaled,
            *shares,
        )
        parts.append(part)
    outs = call(
        functools.partial(token_bwd, count, groups),
        [struct((2,) + back.shape, BF16)] * count,
        [pltpu.VMEM(column, F32), pltpu.VMEM(column, F32)],
        *parts,
        normed,
        inv_std,
        temporal_kernel,
        norm_gain,
        w_expand,
        branch,
    )
    arrived = to_frames(list(outs))

    block_out, grad_clips = call(
        functools.partial(spatial_bwd, count),
        [struct(clips.shape, BF16)] * 2,
        [pad],
        *arrived,
        clips,
        cotangent,
        spatial_kernel,
    )
    if staged:
        grad_expand = scatter_grad(*shares, count, scale_factor, outs[0])
    else:
        whole = lax.dot_general(
            parts[0], scaled, (((0,), (0,)), ((), ())), preferred_element_type=F32
        )
        whole = lax.psum_scatter(whole, ("tm", "dp"), scatter_dimension=0, tiled=True)
        grad_expand = whole * scale_factor
    return (block_out, grad_clips, grad_expand)


def solution(mesh):
    in_specs = (
        P(("groups", "dp"), "tm", None, None, None),
        P(("groups", "dp"), "tm", None, None, None),
        P(),
        P(),
        P(),
        P(),
        P(),
    )
    out_specs = (
        P(("groups", "dp"), "tm", None, None, None),
        P(("groups", "dp"), "tm", None, None, None),
        P(("groups", "tm", "dp"), None),
    )
    return jax.shard_map(local, mesh=mesh, in_specs=in_specs, out_specs=out_specs, check_vma=False)
```

```python
import functools
import jax
import jax.numpy as jnp
from jax import lax
from jax.experimental import pallas as pl
from jax.experimental.pallas import tpu as pltpu
from jax.sharding import PartitionSpec as P

LANES = 128
PAD = 8
F32 = jnp.float32
BF16 = jnp.bfloat16
VMEM_LIMIT = 32 * 1024 * 1024


def call(body, outs, scratch, *args, cost=0, far=0, wait=(), limit=VMEM_LIMIT):
    specs = [pl.BlockSpec(memory_space=pltpu.HBM)] * far
    specs += [pl.BlockSpec(memory_space=pltpu.VMEM)] * (len(args) - far)
    args = [
        pltpu.with_memory_space_constraint(a, pltpu.HBM) if i < far else a
        for i, a in enumerate(args)
    ]
    given = len(args)
    for a in wait:
        specs.append(pl.BlockSpec(memory_space=pl.ANY))
        args.append(pltpu.with_memory_space_constraint(a, pltpu.HBM) if a.ndim == 5 else a)

    def kernel(*refs):
        body(*refs[:given], *refs[given + len(wait) :])

    return pl.pallas_call(
        kernel,
        out_shape=tuple(outs),
        in_specs=specs,
        out_specs=tuple([pl.BlockSpec(memory_space=pltpu.VMEM)] * len(outs)),
        scratch_shapes=list(scratch),
        cost_estimate=pl.CostEstimate(flops=cost, bytes_accessed=cost, transcendentals=0),
        compiler_params=pltpu.CompilerParams(vmem_limit_bytes=limit),
    )(*args)


def struct(shape, dtype):
    return jax.ShapeDtypeStruct(tuple(shape), dtype)


def slot_to(step, count):
    if count == 1:
        return 0
    return lax.rem(lax.axis_index("tm") + step, count)


def slot_from(step, count):
    if count == 1:
        return 0
    return lax.rem(lax.axis_index("tm") + count - step, count)


def partner(step, count):
    if count == 1:
        return 0
    return lax.bitwise_xor(lax.axis_index("tm"), step)


def swap(pieces):
    got = [pieces[0]]
    for step in range(1, len(pieces)):
        pairs = [(i, i ^ step) for i in range(len(pieces))]
        got.append(lax.ppermute(pieces[step], "tm", pairs))
    return got


def exchange(pieces):
    count = len(pieces)
    got = [pieces[0]]
    for step in range(1, count):
        pairs = [(i, (i + step) % count) for i in range(count)]
        got.append(lax.ppermute(pieces[step], "tm", pairs))
    return got


def conv_rows(pad_ref, kernel_ref, block, col, height, flip, emit, low=0, high=None):
    taps = kernel_ref.shape[0]
    lanes = slice(block * LANES, (block + 1) * LANES)
    radius = taps // 2
    high = height if high is None else high
    acc = [None] * height
    for col_off in range(taps):
        shift = radius - col_off if flip else col_off - radius
        weights = [
            kernel_ref[row_off, pl.ds(col_off, 1), lanes] for row_off in range(taps)
        ]
        for row in range(max(low - radius, 0), min(high + radius, height)):
            values = pad_ref[block, :, row, pl.ds(PAD + col + shift, 8), :]
            for row_off in range(taps):
                out = row - radius + row_off if flip else row + radius - row_off
                if low <= out < high:
                    term = values * weights[row_off][None]
                    acc[out] = term if acc[out] is None else acc[out] + term
    for row in range(low, high):
        emit(row, acc[row])


def clear_pads(pad_ref, width):
    blocks, frames, height, _, lanes = pad_ref.shape
    zero = jnp.zeros((blocks, frames, height, PAD, lanes), F32)
    pad_ref[:, :, :, 0:PAD, :] = zero
    pad_ref[:, :, :, PAD + width : PAD + width + PAD, :] = zero


def spatial_fwd(count, *refs):
    clips_far, cot_far, kernel_far = refs[:3]
    held = (len(refs) - 3 - 2 * count - 5) // 2
    fars = refs[3 : 3 + held]
    refs = refs[3 + held :]
    firsts = refs[:count]
    cots = refs[count : 2 * count]
    nears = refs[2 * count : 2 * count + held]
    clips, kernel, pad_ref, flat, sems = refs[2 * count + held :]
    frames, height, width, channels = clips.shape
    blocks = channels // LANES
    pixels = height * width // count
    rows = height // count
    copies = [
        pltpu.make_async_copy(clips_far.at[0], clips, sems.at[0]),
        pltpu.make_async_copy(kernel_far, kernel, sems.at[1]),
    ]
    for step in range(count):
        base = slot_to(step, count) * rows
        copies.append(
            pltpu.make_async_copy(
                cot_far.at[0, :, pl.ds(base, rows)], cots[step], sems.at[2 + step]
            )
        )
    for index in range(held):
        copies.append(
            pltpu.make_async_copy(fars[index], nears[index], sems.at[2 + count + index])
        )
    for copy in copies:
        copy.start()
    clear_pads(pad_ref, width)
    copies[0].wait()
    for block in range(blocks):
        lanes = slice(block * LANES, (block + 1) * LANES)
        pad_ref[block, :, :, PAD : PAD + width, :] = clips[:, :, :, lanes].astype(F32)
    copies[1].wait()
    for block in range(blocks):
        lanes = slice(block * LANES, (block + 1) * LANES)
        for col in range(0, width, 8):

            def emit(row, value):
                flat[:, row, pl.ds(col, 8), lanes] = value

            conv_rows(pad_ref, kernel, block, col, height, False, emit)
    for step in range(count):
        base = partner(step, count) * rows
        firsts[step][...] = (
            flat[:, pl.ds(base, rows), :, :].reshape(frames, pixels, channels).astype(BF16)
        )
    for copy in copies[2:]:
        copy.wait()


def half_rows(pad_ref, kernel, flat, half):
    blocks, _, height, padded, _ = pad_ref.shape
    for value in range(2):
        low = value * height // 2

        @pl.when(half == value)
        def _():
            for block in range(blocks):
                lanes = slice(block * LANES, (block + 1) * LANES)
                for col in range(0, padded - 2 * PAD, 8):

                    def emit(row, result):
                        flat[:, row - low, pl.ds(col, 8), lanes] = result

                    conv_rows(
                        pad_ref, kernel, block, col, height, False, emit, low, low + height // 2
                    )


def spatial_far(clips_far, kernel_far, first_a, first_b, pad_ref, kernel, clips, flat, sems):
    frames, height, width, channels = clips.shape
    copies = [
        pltpu.make_async_copy(clips_far.at[0], clips, sems.at[0]),
        pltpu.make_async_copy(kernel_far, kernel, sems.at[1]),
    ]
    for copy in copies:
        copy.start()
    clear_pads(pad_ref, width)
    copies[0].wait()
    for block in range(channels // LANES):
        lanes = slice(block * LANES, (block + 1) * LANES)
        pad_ref[block, :, :, PAD : PAD + width, :] = clips[:, :, :, lanes].astype(F32)
    copies[1].wait()
    half = 1 - lax.div(lax.axis_index("tm"), 2)
    half_rows(pad_ref, kernel, flat, half)
    rows = height // 4
    for step, out in ((2, first_a), (3, first_b)):
        base = partner(step, 4) * rows - half * (height // 2)
        out[...] = flat[:, pl.ds(base, rows)].reshape(out.shape).astype(BF16)


def spatial_near(held, *refs):
    cot_far, fars = refs[0], refs[1 : 1 + held]
    pad_ref, kernel, first_own, first_near = refs[1 + held : 5 + held]
    cots, nears = refs[5 + held : 9 + held], refs[9 + held : 9 + 2 * held]
    flat, sems = refs[9 + 2 * held :]
    height = pad_ref.shape[2]
    rows = height // 4
    copies = []
    for step in range(4):
        base = slot_to(step, 4) * rows
        copies.append(
            pltpu.make_async_copy(cot_far.at[0, :, pl.ds(base, rows)], cots[step], sems.at[step])
        )
    for index in range(held):
        copies.append(pltpu.make_async_copy(fars[index], nears[index], sems.at[4 + index]))
    for copy in copies:
        copy.start()
    half = lax.div(lax.axis_index("tm"), 2)
    half_rows(pad_ref, kernel, flat, half)
    for step, out in ((0, first_own), (1, first_near)):
        base = partner(step, 4) * rows - half * (height // 2)
        out[...] = flat[:, pl.ds(base, rows)].reshape(out.shape).astype(BF16)
    for copy in copies:
        copy.wait()


def spatial_bwd(count, *refs):
    pieces = refs[:count]
    clips, cot, kernel, block_out, out_ref, pad_ref = refs[count:]
    _, frames, height, width, channels = cot.shape
    blocks = channels // LANES
    rows = height // count
    clear_pads(pad_ref, width)
    for step in range(count):
        base = partner(step, count) * rows
        for block in range(blocks):
            lanes = slice(block * LANES, (block + 1) * LANES)
            piece = pieces[step][1, :, :, lanes].astype(F32).reshape(frames, rows, width, LANES)
            pad_ref[block, :, pl.ds(base, rows), PAD : PAD + width, :] = piece
        here = (0, slice(None), pl.ds(base, rows))
        branch = pieces[step][0].reshape(frames, rows, width, channels).astype(F32)
        block_out[here] = (clips[here].astype(F32) + branch).astype(BF16)
    for block in range(blocks):
        lanes = slice(block * LANES, (block + 1) * LANES)
        for col in range(0, width, 16):
            halves = []
            for part in range(2):
                rows_out = []
                conv_rows(
                    pad_ref, kernel, block, col + 8 * part, height, True,
                    lambda row, value: rows_out.append(value),
                )
                halves.append(rows_out)
            for row in range(height):
                total = jnp.concatenate([halves[0][row], halves[1][row]], axis=1)
                total = total + cot[0, :, row, pl.ds(col, 16), lanes].astype(F32)
                out_ref[0, :, row, pl.ds(col, 16), lanes] = total.astype(BF16)


def mix_frames(source, target, kernel, flip):
    frames = source.shape[0]
    taps = kernel.shape[0]
    radius = taps // 2
    if frames <= 16:
        for out in range(frames):
            total = None
            for inp in range(frames):
                lag = (out - inp if flip else inp - out) + radius
                if 0 <= lag < taps:
                    term = kernel[pl.ds(lag, 1), :] * source[inp]
                    total = term if total is None else total + term
            target[out] = total.astype(BF16).astype(F32)
        return

    def one(out, carry):
        def tap(inp, total):
            lag = (out - inp if flip else inp - out) + radius
            return total + kernel[pl.ds(lag, 1), :] * source[inp]

        low = jnp.maximum(out - radius, 0)
        high = jnp.minimum(out + radius + 1, frames)
        total = lax.fori_loop(low, high, tap, jnp.zeros(source.shape[1:], F32))
        target[out] = total.astype(BF16).astype(F32)
        return carry

    lax.fori_loop(0, frames, one, 0)


def place_frames(count, pieces, target):
    for step in range(count):
        frames = pieces[step].shape[0]
        base = partner(step, count) * frames
        piece = pieces[step][...].reshape((frames,) + target.shape[1:])
        target[pl.ds(base, frames)] = piece.astype(target.dtype)


def mlp_fwd(count, chunk, *refs):
    pieces = refs[:count]
    taps, gain, w_expand, w_project = refs[count : count + 4]
    branch, scaled, slope, normed, inv_std, mixed_in, mixed, hidden = refs[count + 4 :]
    frames, pixels, channels = mixed_in.shape
    tokens = frames * pixels
    place_frames(count, pieces, mixed_in)
    mix_frames(mixed_in, mixed, taps, False)
    values = mixed[...].reshape(tokens, channels)
    average = jnp.mean(values, axis=-1, keepdims=True)
    centred = values - average
    inverse = lax.rsqrt(jnp.mean(centred * centred, axis=-1, keepdims=True) + 1e-06)
    inv_std[...] = inverse
    norm = centred * inverse
    normed[...] = norm
    scaled[...] = (norm * gain[...].reshape(1, channels)).astype(BF16)
    for start in range(0, w_expand.shape[1], chunk):
        part = slice(start, start + chunk)
        pre = jnp.dot(scaled[...], w_expand[:, part], preferred_element_type=F32)
        cdf = 0.5 + 0.5 * lax.erf(pre * 0.7071067811865476)
        hidden[:, part] = (pre * cdf).astype(BF16)
        slope[:, part] = (cdf + pre * jnp.exp(-0.5 * pre * pre) * 0.3989422804014327).astype(BF16)
    out = jnp.dot(hidden[...], w_project[...], preferred_element_type=F32).astype(BF16)
    branch[...] = out.reshape(branch.shape)


def hidden_bwd(count, steps, with_grad, final, *refs):
    pieces = refs[: len(steps)]
    slope, w_project, scaled = refs[len(steps) : len(steps) + 3]
    refs = refs[len(steps) + 3 :]
    channels = scaled.shape[1]
    rows = scaled.shape[0] // count
    sources = [pl.multiple_of(slot_from(step, count) * rows, rows) for step in steps]
    grads = jnp.concatenate([p[...].reshape(rows, channels) for p in pieces], axis=0)
    d_hidden = lax.dot_general(
        grads, w_project[...], (((1,), (1,)), ((), ())), preferred_element_type=F32
    )
    steep = jnp.concatenate([slope[pl.ds(source, rows), :] for source in sources], axis=0)
    result = (d_hidden * steep.astype(F32)).astype(BF16)
    if not (with_grad and final):
        refs[-1][...] = result
        return
    before, d_pre, keep, send, full = refs
    d_pre[...] = result
    order = [step for step in range(count) if step not in steps] + list(steps)
    sources = [pl.multiple_of(slot_from(step, count) * rows, rows) for step in order]
    inputs = jnp.concatenate([scaled[pl.ds(source, rows), :] for source in sources], axis=0)
    both = jnp.concatenate([before[...], result], axis=0)
    share = lax.dot_general(both, inputs, (((0,), (0,)), ((), ())), preferred_element_type=F32)
    full[...] = share.reshape(full.shape)
    core = lax.rem(lax.axis_index("dp"), 2)
    for pair in range(full.shape[0] // 2):
        keep[pair] = full[2 * pair + core]
        send[pair] = full[2 * pair + 1 - core].astype(BF16)


def token_bwd(count, groups, *refs):
    parts, refs = refs[: len(groups)], refs[len(groups) :]
    normed, inv_std, taps, gain, w_expand, branch = refs[:6]
    outs = refs[6 : count + 6]
    d_second, d_first = refs[count + 6 :]
    frames, pixels, channels = d_second.shape
    own = frames // count
    last = (((1,), (1,)), ((), ()))
    for steps, d_pre in zip(groups, parts):
        d_scaled = lax.dot_general(d_pre[...], w_expand[...], last, preferred_element_type=F32)
        d_scaled = d_scaled.reshape(len(steps), own, pixels, channels)
        for index, step in enumerate(steps):
            d_second[pl.ds(slot_from(step, count) * own, own)] = d_scaled[index]
    d_normed = d_second[...].reshape(frames * pixels, channels) * gain[...].reshape(1, channels)
    norm = normed[...]
    d_tokens = inv_std[...] * (
        d_normed
        - jnp.mean(d_normed, axis=-1, keepdims=True)
        - norm * jnp.mean(d_normed * norm, axis=-1, keepdims=True)
    )
    d_second[...] = d_tokens.astype(BF16).astype(F32).reshape(frames, pixels, channels)
    mix_frames(d_second, d_first, taps, True)
    for step in range(count):
        base = partner(step, count) * own
        outs[step][0] = branch[pl.ds(base, own)]
        outs[step][1] = d_first[pl.ds(base, own)].astype(BF16)


def fold_pair(keep_in, got, keep, send):
    side = lax.div(lax.axis_index("dp"), 2)
    for slot in range(keep.shape[0]):
        mine, other = 2 * slot + side, 2 * slot + 1 - side
        keep[slot] = keep_in[mine] + got[mine].astype(F32)
        send[slot] = (keep_in[other] + got[other].astype(F32)).astype(BF16)


def fold_near(keep_in, got, keep, *sends):
    me = lax.axis_index("tm")
    for far in range(2):
        mine = lax.bitwise_xor(me, 2 * far)
        other = lax.bitwise_xor(me, 2 * far + 1)
        keep[far] = keep_in[mine] + got[mine].astype(F32)
        sends[far][...] = (keep_in[other] + got[other].astype(F32)).astype(BF16)


def fold_far(keep_in, got, got_far, keep, send):
    keep[...] = keep_in[0] + got[...].astype(F32)
    send[...] = (keep_in[1] + got_far[...].astype(F32)).astype(BF16)


def fold_last(scale_factor, keep_in, *refs):
    total = keep_in[...]
    for got in refs[:-1]:
        total = total + got[...].astype(F32)
    refs[-1][...] = total * scale_factor


def scatter_grad(keep, send, count, scale_factor, d_first):
    channels = keep.shape[-1]
    block = keep.shape[1]
    quarter = (count, block, channels)
    piece = (block, channels)
    got = lax.ppermute(send, "dp", [(i, i ^ 1) for i in range(4)])
    keep, send = call(
        fold_pair, [struct(quarter, F32), struct(quarter, BF16)], [], keep, got, wait=[d_first]
    )
    got = lax.ppermute(send, "dp", [(i, i ^ 2) for i in range(4)])
    pair = (2,) + piece
    keep, *sends = call(
        fold_near, [struct(pair, F32), struct(piece, BF16), struct(piece, BF16)], [], keep, got
    )
    near = [lax.ppermute(send, "tm", [(i, i ^ 1) for i in range(4)]) for send in sends]
    keep, send = call(
        fold_far, [struct(piece, F32), struct(piece, BF16)], [], keep, *near
    )
    got = lax.ppermute(send, "tm", [(i, i ^ 2) for i in range(4)])
    return call(functools.partial(fold_last, scale_factor), [struct(piece, F32)], [], keep, got)[0]


def local(clips, cotangent, spatial_kernel, temporal_kernel, norm_gain, w_expand, w_project):
    _, frames, height, width, channels = clips.shape
    members = lax.axis_size("tm")
    device_count = members * lax.axis_size("dp")
    pixels = height * width
    scale_factor = float(clips.shape[0] * frames * pixels * device_count) ** (-0.5)
    hid = w_expand.shape[1]
    chunk = 256
    blocks = channels // LANES
    count = members if members in (2, 4, 8) and height % members == 0 else 1
    all_frames = frames * members
    columns = pixels // members
    tokens = all_frames * columns

    def to_columns(pieces):
        if count > 1:
            return exchange(pieces)
        whole = pieces[0].reshape(1, frames, pixels, channels)
        return [lax.all_to_all(whole, "tm", split_axis=2, concat_axis=1, tiled=True)[0]]

    def to_frames(pieces):
        if count > 1:
            return swap(pieces)
        return [lax.all_to_all(pieces[0], "tm", split_axis=1, concat_axis=2, tiled=True)]

    pad = pltpu.VMEM((blocks, frames, height, width + 2 * PAD, LANES), F32)
    piece = struct((frames, pixels // count, channels), BF16)
    cot_piece = struct((frames, height // count, width, channels), BF16)
    held = [temporal_kernel, w_expand, w_project]
    kept = [struct(a.shape, a.dtype) for a in held]
    image = (frames, height, width, channels)
    if count == 4:
        half_image = pltpu.VMEM((frames, height // 2, width, channels), F32)
        *far, padded, taps = call(
            spatial_far,
            [piece] * 2 + [struct(pad.shape, F32), struct(spatial_kernel.shape, F32)],
            [pltpu.VMEM(image, BF16), half_image, pltpu.SemaphoreType.DMA((2,))],
            clips,
            spatial_kernel,
            far=2,
        )
        outs = call(
            functools.partial(spatial_near, len(held)),
            [piece] * 2 + [cot_piece] * count + kept,
            [half_image, pltpu.SemaphoreType.DMA((count + len(held),))],
            cotangent,
            *held,
            padded,
            taps,
            far=1 + len(held),
        )
        outs = [outs[0], outs[1], *far, *outs[2:]]
    else:
        outs = call(
            functools.partial(spatial_fwd, count),
            [piece] * count + [cot_piece] * count + [struct(a.shape, a.dtype) for a in held],
            [
                pltpu.VMEM(clips.shape[1:], BF16),
                pltpu.VMEM(spatial_kernel.shape, F32),
                pad,
                pltpu.VMEM((frames, height, width, channels), F32),
                pltpu.SemaphoreType.DMA((2 + count + len(held),)),
            ],
            clips,
            cotangent,
            spatial_kernel,
            *held,
            far=3 + len(held),
        )
    firsts = swap(outs[:count]) if count > 1 else to_columns(list(outs[:count]))
    cots = to_columns(list(outs[count : 2 * count]))
    temporal_kernel, w_expand, w_project = outs[2 * count :]

    column = (all_frames, columns, channels)
    back = struct((all_frames // count, columns, channels), BF16)
    outs = call(
        functools.partial(mlp_fwd, count, chunk),
        [
            struct(column, BF16),
            struct((tokens, channels), BF16),
            struct((tokens, hid), BF16),
            struct((tokens, channels), F32),
            struct((tokens, 1), F32),
        ],
        [
            pltpu.VMEM(column, F32),
            pltpu.VMEM(column, F32),
            pltpu.VMEM((tokens, hid), BF16),
        ],
        *firsts,
        temporal_kernel,
        norm_gain,
        w_expand,
        w_project,
    )
    branch, scaled, slope, normed, inv_std = outs

    sides = lax.axis_size("dp")
    staged = count == 4 and sides == 4
    half = (2 * count, hid // (sides * count), channels)
    whole = (2 * half[0],) + half[1:]
    groups = [[0, 1], [2, 3]] if staged else [list(range(count))]
    parts, shares = [], []
    for steps in groups:
        rows = len(steps) * tokens // count
        final = steps is groups[-1]
        results = [struct((rows, hid), BF16)]
        if staged and final:
            results += [struct(half, F32), struct(half, BF16)]
        part, *shares = call(
            functools.partial(hidden_bwd, count, steps, staged, final),
            results,
            [pltpu.VMEM(whole, F32)] if staged and final else [],
            *[cots[step] for step in steps],
            slope,
            w_project,
            scaled,
            *parts,
        )
        parts.append(part)
    outs = call(
        functools.partial(token_bwd, count, groups),
        [struct((2,) + back.shape, BF16)] * count,
        [pltpu.VMEM(column, F32), pltpu.VMEM(column, F32)],
        *parts,
        normed,
        inv_std,
        temporal_kernel,
        norm_gain,
        w_expand,
        branch,
    )
    arrived = to_frames(list(outs))

    block_out, grad_clips = call(
        functools.partial(spatial_bwd, count),
        [struct(clips.shape, BF16)] * 2,
        [pad],
        *arrived,
        clips,
        cotangent,
        spatial_kernel,
    )
    if staged:
        grad_expand = scatter_grad(*shares, count, scale_factor, outs[0])
    else:
        whole = lax.dot_general(
            parts[0], scaled, (((0,), (0,)), ((), ())), preferred_element_type=F32
        )
        whole = lax.psum_scatter(whole, ("tm", "dp"), scatter_dimension=0, tiled=True)
        grad_expand = whole * scale_factor
    return (block_out, grad_clips, grad_expand)


def solution(mesh):
    in_specs = (
        P(("groups", "dp"), "tm", None, None, None),
        P(("groups", "dp"), "tm", None, None, None),
        P(),
        P(),
        P(),
        P(),
        P(),
    )
    out_specs = (
        P(("groups", "dp"), "tm", None, None, None),
        P(("groups", "dp"), "tm", None, None, None),
        P(("groups", "tm", "dp"), None),
    )
    return jax.shard_map(local, mesh=mesh, in_specs=in_specs, out_specs=out_specs, check_vma=False)
```

```python
import functools
import jax
import jax.numpy as jnp
from jax import lax
from jax.experimental import pallas as pl
from jax.experimental.pallas import tpu as pltpu
from jax.sharding import PartitionSpec as P

LANES = 128
PAD = 8
F32 = jnp.float32
BF16 = jnp.bfloat16
VMEM_LIMIT = 32 * 1024 * 1024


def call(body, outs, scratch, *args, cost=0, far=0, wait=(), limit=VMEM_LIMIT):
    specs = [pl.BlockSpec(memory_space=pltpu.HBM)] * far
    specs += [pl.BlockSpec(memory_space=pltpu.VMEM)] * (len(args) - far)
    args = [
        pltpu.with_memory_space_constraint(a, pltpu.HBM) if i < far else a
        for i, a in enumerate(args)
    ]
    given = len(args)
    for a in wait:
        specs.append(pl.BlockSpec(memory_space=pl.ANY))
        args.append(pltpu.with_memory_space_constraint(a, pltpu.HBM) if a.ndim == 5 else a)

    def kernel(*refs):
        body(*refs[:given], *refs[given + len(wait) :])

    return pl.pallas_call(
        kernel,
        out_shape=tuple(outs),
        in_specs=specs,
        out_specs=tuple([pl.BlockSpec(memory_space=pltpu.VMEM)] * len(outs)),
        scratch_shapes=list(scratch),
        cost_estimate=pl.CostEstimate(flops=cost, bytes_accessed=cost, transcendentals=0),
        compiler_params=pltpu.CompilerParams(vmem_limit_bytes=limit),
    )(*args)


def struct(shape, dtype):
    return jax.ShapeDtypeStruct(tuple(shape), dtype)


def slot_to(step, count):
    if count == 1:
        return 0
    return lax.rem(lax.axis_index("tm") + step, count)


def slot_from(step, count):
    if count == 1:
        return 0
    return lax.rem(lax.axis_index("tm") + count - step, count)


def partner(step, count):
    if count == 1:
        return 0
    return lax.bitwise_xor(lax.axis_index("tm"), step)


def swap(pieces):
    got = [pieces[0]]
    for step in range(1, len(pieces)):
        pairs = [(i, i ^ step) for i in range(len(pieces))]
        got.append(lax.ppermute(pieces[step], "tm", pairs))
    return got


def exchange(pieces):
    count = len(pieces)
    got = [pieces[0]]
    for step in range(1, count):
        pairs = [(i, (i + step) % count) for i in range(count)]
        got.append(lax.ppermute(pieces[step], "tm", pairs))
    return got


def conv_rows(pad_ref, kernel_ref, block, col, height, flip, emit, low=0, high=None):
    taps = kernel_ref.shape[0]
    lanes = slice(block * LANES, (block + 1) * LANES)
    radius = taps // 2
    high = height if high is None else high
    acc = [None] * height
    for col_off in range(taps):
        shift = radius - col_off if flip else col_off - radius
        weights = [
            kernel_ref[row_off, pl.ds(col_off, 1), lanes] for row_off in range(taps)
        ]
        for row in range(max(low - radius, 0), min(high + radius, height)):
            values = pad_ref[block, :, row, pl.ds(PAD + col + shift, 8), :]
            for row_off in range(taps):
                out = row - radius + row_off if flip else row + radius - row_off
                if low <= out < high:
                    term = values * weights[row_off][None]
                    acc[out] = term if acc[out] is None else acc[out] + term
    for row in range(low, high):
        emit(row, acc[row])


def clear_pads(pad_ref, width):
    blocks, frames, height, _, lanes = pad_ref.shape
    zero = jnp.zeros((blocks, frames, height, PAD, lanes), F32)
    pad_ref[:, :, :, 0:PAD, :] = zero
    pad_ref[:, :, :, PAD + width : PAD + width + PAD, :] = zero


def spatial_fwd(count, *refs):
    clips_far, cot_far, kernel_far = refs[:3]
    held = (len(refs) - 3 - 2 * count - 5) // 2
    fars = refs[3 : 3 + held]
    refs = refs[3 + held :]
    firsts = refs[:count]
    cots = refs[count : 2 * count]
    nears = refs[2 * count : 2 * count + held]
    clips, kernel, pad_ref, flat, sems = refs[2 * count + held :]
    frames, height, width, channels = clips.shape
    blocks = channels // LANES
    pixels = height * width // count
    rows = height // count
    copies = [
        pltpu.make_async_copy(clips_far.at[0], clips, sems.at[0]),
        pltpu.make_async_copy(kernel_far, kernel, sems.at[1]),
    ]
    for step in range(count):
        base = slot_to(step, count) * rows
        copies.append(
            pltpu.make_async_copy(
                cot_far.at[0, :, pl.ds(base, rows)], cots[step], sems.at[2 + step]
            )
        )
    for index in range(held):
        copies.append(
            pltpu.make_async_copy(fars[index], nears[index], sems.at[2 + count + index])
        )
    for copy in copies:
        copy.start()
    clear_pads(pad_ref, width)
    copies[0].wait()
    for block in range(blocks):
        lanes = slice(block * LANES, (block + 1) * LANES)
        pad_ref[block, :, :, PAD : PAD + width, :] = clips[:, :, :, lanes].astype(F32)
    copies[1].wait()
    for block in range(blocks):
        lanes = slice(block * LANES, (block + 1) * LANES)
        for col in range(0, width, 8):

            def emit(row, value):
                flat[:, row, pl.ds(col, 8), lanes] = value

            conv_rows(pad_ref, kernel, block, col, height, False, emit)
    for step in range(count):
        base = partner(step, count) * rows
        firsts[step][...] = (
            flat[:, pl.ds(base, rows), :, :].reshape(frames, pixels, channels).astype(BF16)
        )
    for copy in copies[2:]:
        copy.wait()


def half_rows(pad_ref, kernel, flat, half):
    blocks, _, height, padded, _ = pad_ref.shape
    for value in range(2):
        low = value * height // 2

        @pl.when(half == value)
        def _():
            for block in range(blocks):
                lanes = slice(block * LANES, (block + 1) * LANES)
                for col in range(0, padded - 2 * PAD, 8):

                    def emit(row, result):
                        flat[:, row - low, pl.ds(col, 8), lanes] = result

                    conv_rows(
                        pad_ref, kernel, block, col, height, False, emit, low, low + height // 2
                    )


def spatial_far(clips_far, kernel_far, first_a, first_b, pad_ref, kernel, clips, flat, sems):
    frames, height, width, channels = clips.shape
    copies = [
        pltpu.make_async_copy(clips_far.at[0], clips, sems.at[0]),
        pltpu.make_async_copy(kernel_far, kernel, sems.at[1]),
    ]
    for copy in copies:
        copy.start()
    clear_pads(pad_ref, width)
    copies[0].wait()
    for block in range(channels // LANES):
        lanes = slice(block * LANES, (block + 1) * LANES)
        pad_ref[block, :, :, PAD : PAD + width, :] = clips[:, :, :, lanes].astype(F32)
    copies[1].wait()
    half = 1 - lax.div(lax.axis_index("tm"), 2)
    half_rows(pad_ref, kernel, flat, half)
    rows = height // 4
    for step, out in ((2, first_a), (3, first_b)):
        base = partner(step, 4) * rows - half * (height // 2)
        out[...] = flat[:, pl.ds(base, rows)].reshape(out.shape).astype(BF16)


def spatial_near(held, *refs):
    cot_far, fars = refs[0], refs[1 : 1 + held]
    pad_ref, kernel, first_own, first_near = refs[1 + held : 5 + held]
    cots, nears = refs[5 + held : 9 + held], refs[9 + held : 9 + 2 * held]
    flat, sems = refs[9 + 2 * held :]
    height = pad_ref.shape[2]
    rows = height // 4
    copies = []
    for step in range(4):
        base = slot_to(step, 4) * rows
        copies.append(
            pltpu.make_async_copy(cot_far.at[0, :, pl.ds(base, rows)], cots[step], sems.at[step])
        )
    for index in range(held):
        copies.append(pltpu.make_async_copy(fars[index], nears[index], sems.at[4 + index]))
    for copy in copies:
        copy.start()
    half = lax.div(lax.axis_index("tm"), 2)
    half_rows(pad_ref, kernel, flat, half)
    for step, out in ((0, first_own), (1, first_near)):
        base = partner(step, 4) * rows - half * (height // 2)
        out[...] = flat[:, pl.ds(base, rows)].reshape(out.shape).astype(BF16)
    for copy in copies:
        copy.wait()


def spatial_bwd(count, *refs):
    pieces = refs[:count]
    clips, cot, kernel, block_out, out_ref, pad_ref = refs[count:]
    _, frames, height, width, channels = cot.shape
    blocks = channels // LANES
    rows = height // count
    clear_pads(pad_ref, width)
    for step in range(count):
        base = partner(step, count) * rows
        for block in range(blocks):
            lanes = slice(block * LANES, (block + 1) * LANES)
            piece = pieces[step][1, :, :, lanes].astype(F32).reshape(frames, rows, width, LANES)
            pad_ref[block, :, pl.ds(base, rows), PAD : PAD + width, :] = piece
        here = (0, slice(None), pl.ds(base, rows))
        branch = pieces[step][0].reshape(frames, rows, width, channels).astype(F32)
        block_out[here] = (clips[here].astype(F32) + branch).astype(BF16)
    for block in range(blocks):
        lanes = slice(block * LANES, (block + 1) * LANES)
        for col in range(0, width, 16):
            halves = []
            for part in range(2):
                rows_out = []
                conv_rows(
                    pad_ref, kernel, block, col + 8 * part, height, True,
                    lambda row, value: rows_out.append(value),
                )
                halves.append(rows_out)
            for row in range(height):
                total = jnp.concatenate([halves[0][row], halves[1][row]], axis=1)
                total = total + cot[0, :, row, pl.ds(col, 16), lanes].astype(F32)
                out_ref[0, :, row, pl.ds(col, 16), lanes] = total.astype(BF16)


def mix_frames(source, target, kernel, flip):
    frames = source.shape[0]
    taps = kernel.shape[0]
    radius = taps // 2
    if frames <= 16:
        for out in range(frames):
            total = None
            for inp in range(frames):
                lag = (out - inp if flip else inp - out) + radius
                if 0 <= lag < taps:
                    term = kernel[pl.ds(lag, 1), :] * source[inp]
                    total = term if total is None else total + term
            target[out] = total.astype(BF16).astype(F32)
        return

    def one(out, carry):
        def tap(inp, total):
            lag = (out - inp if flip else inp - out) + radius
            return total + kernel[pl.ds(lag, 1), :] * source[inp]

        low = jnp.maximum(out - radius, 0)
        high = jnp.minimum(out + radius + 1, frames)
        total = lax.fori_loop(low, high, tap, jnp.zeros(source.shape[1:], F32))
        target[out] = total.astype(BF16).astype(F32)
        return carry

    lax.fori_loop(0, frames, one, 0)


def place_frames(count, pieces, target):
    for step in range(count):
        frames = pieces[step].shape[0]
        base = partner(step, count) * frames
        piece = pieces[step][...].reshape((frames,) + target.shape[1:])
        target[pl.ds(base, frames)] = piece.astype(target.dtype)


def mlp_fwd(count, chunk, *refs):
    pieces = refs[:count]
    taps, gain, w_expand, w_project = refs[count : count + 4]
    branch, scaled, slope, normed, inv_std, mixed_in, mixed, hidden = refs[count + 4 :]
    frames, pixels, channels = mixed_in.shape
    tokens = frames * pixels
    place_frames(count, pieces, mixed_in)
    mix_frames(mixed_in, mixed, taps, False)
    values = mixed[...].reshape(tokens, channels)
    average = jnp.mean(values, axis=-1, keepdims=True)
    centred = values - average
    inverse = lax.rsqrt(jnp.mean(centred * centred, axis=-1, keepdims=True) + 1e-06)
    inv_std[...] = inverse
    norm = centred * inverse
    normed[...] = norm
    scaled[...] = (norm * gain[...].reshape(1, channels)).astype(BF16)
    for start in range(0, w_expand.shape[1], chunk):
        part = slice(start, start + chunk)
        pre = jnp.dot(scaled[...], w_expand[:, part], preferred_element_type=F32)
        cdf = 0.5 + 0.5 * lax.erf(pre * 0.7071067811865476)
        hidden[:, part] = (pre * cdf).astype(BF16)
        slope[:, part] = (cdf + pre * jnp.exp(-0.5 * pre * pre) * 0.3989422804014327).astype(BF16)
    out = jnp.dot(hidden[...], w_project[...], preferred_element_type=F32).astype(BF16)
    branch[...] = out.reshape(branch.shape)


def hidden_bwd(count, steps, with_grad, final, *refs):
    pieces = refs[: len(steps)]
    slope, w_project, scaled = refs[len(steps) : len(steps) + 3]
    refs = refs[len(steps) + 3 :]
    channels = scaled.shape[1]
    rows = scaled.shape[0] // count
    sources = [pl.multiple_of(slot_from(step, count) * rows, rows) for step in steps]
    grads = jnp.concatenate([p[...].reshape(rows, channels) for p in pieces], axis=0)
    d_hidden = lax.dot_general(
        grads, w_project[...], (((1,), (1,)), ((), ())), preferred_element_type=F32
    )
    steep = jnp.concatenate([slope[pl.ds(source, rows), :] for source in sources], axis=0)
    result = (d_hidden * steep.astype(F32)).astype(BF16)
    if not with_grad:
        refs[-1][...] = result
        return
    inputs = jnp.concatenate([scaled[pl.ds(source, rows), :] for source in sources], axis=0)
    share = lax.dot_general(result, inputs, (((0,), (0,)), ((), ())), preferred_element_type=F32)
    if not final:
        d_pre, full = refs
        d_pre[...] = result
        full[...] = share.reshape(full.shape)
        return
    before, d_pre, keep, send, full = refs
    d_pre[...] = result
    full[...] = share.reshape(full.shape)
    core = lax.rem(lax.axis_index("dp"), 2)
    for pair in range(full.shape[0] // 2):
        mine, other = 2 * pair + core, 2 * pair + 1 - core
        keep[pair] = full[mine] + before[mine]
        send[pair] = (full[other] + before[other]).astype(BF16)


def token_bwd(count, groups, *refs):
    parts, refs = refs[: len(groups)], refs[len(groups) :]
    normed, inv_std, taps, gain, w_expand, branch = refs[:6]
    outs = refs[6 : count + 6]
    d_second, d_first = refs[count + 6 :]
    frames, pixels, channels = d_second.shape
    own = frames // count
    last = (((1,), (1,)), ((), ()))
    for steps, d_pre in zip(groups, parts):
        d_scaled = lax.dot_general(d_pre[...], w_expand[...], last, preferred_element_type=F32)
        d_scaled = d_scaled.reshape(len(steps), own, pixels, channels)
        for index, step in enumerate(steps):
            d_second[pl.ds(slot_from(step, count) * own, own)] = d_scaled[index]
    d_normed = d_second[...].reshape(frames * pixels, channels) * gain[...].reshape(1, channels)
    norm = normed[...]
    d_tokens = inv_std[...] * (
        d_normed
        - jnp.mean(d_normed, axis=-1, keepdims=True)
        - norm * jnp.mean(d_normed * norm, axis=-1, keepdims=True)
    )
    d_second[...] = d_tokens.astype(BF16).astype(F32).reshape(frames, pixels, channels)
    mix_frames(d_second, d_first, taps, True)
    for step in range(count):
        base = partner(step, count) * own
        outs[step][0] = branch[pl.ds(base, own)]
        outs[step][1] = d_first[pl.ds(base, own)].astype(BF16)


def fold_pair(keep_in, got, keep, send):
    side = lax.div(lax.axis_index("dp"), 2)
    for slot in range(keep.shape[0]):
        mine, other = 2 * slot + side, 2 * slot + 1 - side
        keep[slot] = keep_in[mine] + got[mine].astype(F32)
        send[slot] = (keep_in[other] + got[other].astype(F32)).astype(BF16)


def fold_near(keep_in, got, keep, *sends):
    me = lax.axis_index("tm")
    for far in range(2):
        mine = lax.bitwise_xor(me, 2 * far)
        other = lax.bitwise_xor(me, 2 * far + 1)
        keep[far] = keep_in[mine] + got[mine].astype(F32)
        sends[far][...] = (keep_in[other] + got[other].astype(F32)).astype(BF16)


def fold_far(keep_in, got, got_far, keep, send):
    keep[...] = keep_in[0] + got[...].astype(F32)
    send[...] = (keep_in[1] + got_far[...].astype(F32)).astype(BF16)


def fold_last(scale_factor, keep_in, *refs):
    total = keep_in[...]
    for got in refs[:-1]:
        total = total + got[...].astype(F32)
    refs[-1][...] = total * scale_factor


def scatter_grad(keep, send, count, scale_factor, d_first):
    channels = keep.shape[-1]
    block = keep.shape[1]
    quarter = (count, block, channels)
    piece = (block, channels)
    got = lax.ppermute(send, "dp", [(i, i ^ 1) for i in range(4)])
    keep, send = call(
        fold_pair, [struct(quarter, F32), struct(quarter, BF16)], [], keep, got, wait=[d_first]
    )
    got = lax.ppermute(send, "dp", [(i, i ^ 2) for i in range(4)])
    pair = (2,) + piece
    keep, *sends = call(
        fold_near, [struct(pair, F32), struct(piece, BF16), struct(piece, BF16)], [], keep, got
    )
    near = [lax.ppermute(send, "tm", [(i, i ^ 1) for i in range(4)]) for send in sends]
    keep, send = call(
        fold_far, [struct(piece, F32), struct(piece, BF16)], [], keep, *near
    )
    got = lax.ppermute(send, "tm", [(i, i ^ 2) for i in range(4)])
    return call(functools.partial(fold_last, scale_factor), [struct(piece, F32)], [], keep, got)[0]


def local(clips, cotangent, spatial_kernel, temporal_kernel, norm_gain, w_expand, w_project):
    _, frames, height, width, channels = clips.shape
    members = lax.axis_size("tm")
    device_count = members * lax.axis_size("dp")
    pixels = height * width
    scale_factor = float(clips.shape[0] * frames * pixels * device_count) ** (-0.5)
    hid = w_expand.shape[1]
    chunk = 768
    blocks = channels // LANES
    count = members if members in (2, 4, 8) and height % members == 0 else 1
    all_frames = frames * members
    columns = pixels // members
    tokens = all_frames * columns

    def to_columns(pieces):
        if count > 1:
            return exchange(pieces)
        whole = pieces[0].reshape(1, frames, pixels, channels)
        return [lax.all_to_all(whole, "tm", split_axis=2, concat_axis=1, tiled=True)[0]]

    def to_frames(pieces):
        if count > 1:
            return swap(pieces)
        return [lax.all_to_all(pieces[0], "tm", split_axis=1, concat_axis=2, tiled=True)]

    pad = pltpu.VMEM((blocks, frames, height, width + 2 * PAD, LANES), F32)
    piece = struct((frames, pixels // count, channels), BF16)
    cot_piece = struct((frames, height // count, width, channels), BF16)
    held = [temporal_kernel, w_expand, w_project]
    kept = [struct(a.shape, a.dtype) for a in held]
    image = (frames, height, width, channels)
    if count == 4:
        half_image = pltpu.VMEM((frames, height // 2, width, channels), F32)
        *far, padded, taps = call(
            spatial_far,
            [piece] * 2 + [struct(pad.shape, F32), struct(spatial_kernel.shape, F32)],
            [pltpu.VMEM(image, BF16), half_image, pltpu.SemaphoreType.DMA((2,))],
            clips,
            spatial_kernel,
            far=2,
        )
        outs = call(
            functools.partial(spatial_near, len(held)),
            [piece] * 2 + [cot_piece] * count + kept,
            [half_image, pltpu.SemaphoreType.DMA((count + len(held),))],
            cotangent,
            *held,
            padded,
            taps,
            far=1 + len(held),
        )
        outs = [outs[0], outs[1], *far, *outs[2:]]
    else:
        outs = call(
            functools.partial(spatial_fwd, count),
            [piece] * count + [cot_piece] * count + [struct(a.shape, a.dtype) for a in held],
            [
                pltpu.VMEM(clips.shape[1:], BF16),
                pltpu.VMEM(spatial_kernel.shape, F32),
                pad,
                pltpu.VMEM((frames, height, width, channels), F32),
                pltpu.SemaphoreType.DMA((2 + count + len(held),)),
            ],
            clips,
            cotangent,
            spatial_kernel,
            *held,
            far=3 + len(held),
        )
    firsts = swap(outs[:count]) if count > 1 else to_columns(list(outs[:count]))
    cots = to_columns(list(outs[count : 2 * count]))
    temporal_kernel, w_expand, w_project = outs[2 * count :]

    column = (all_frames, columns, channels)
    back = struct((all_frames // count, columns, channels), BF16)
    outs = call(
        functools.partial(mlp_fwd, count, chunk),
        [
            struct(column, BF16),
            struct((tokens, channels), BF16),
            struct((tokens, hid), BF16),
            struct((tokens, channels), F32),
            struct((tokens, 1), F32),
        ],
        [
            pltpu.VMEM(column, F32),
            pltpu.VMEM(column, F32),
            pltpu.VMEM((tokens, hid), BF16),
        ],
        *firsts,
        temporal_kernel,
        norm_gain,
        w_expand,
        w_project,
    )
    branch, scaled, slope, normed, inv_std = outs

    sides = lax.axis_size("dp")
    staged = count == 4 and sides == 4
    half = (2 * count, hid // (sides * count), channels)
    whole = (2 * half[0],) + half[1:]
    groups = [[0, 1], [2, 3]] if staged else [list(range(count))]
    parts, shares = [], []
    for steps in groups:
        rows = len(steps) * tokens // count
        final = steps is groups[-1]
        results = [struct((rows, hid), BF16)]
        if staged and final:
            results += [struct(half, F32), struct(half, BF16)]
        elif staged:
            results += [struct(whole, F32)]
        part, *shares = call(
            functools.partial(hidden_bwd, count, steps, staged, final),
            results,
            [pltpu.VMEM(whole, F32)] if staged and final else [],
            *[cots[step] for step in steps],
            slope,
            w_project,
            scaled,
            *shares,
        )
        parts.append(part)
    outs = call(
        functools.partial(token_bwd, count, groups),
        [struct((2,) + back.shape, BF16)] * count,
        [pltpu.VMEM(column, F32), pltpu.VMEM(column, F32)],
        *parts,
        normed,
        inv_std,
        temporal_kernel,
        norm_gain,
        w_expand,
        branch,
    )
    arrived = to_frames(list(outs))

    block_out, grad_clips = call(
        functools.partial(spatial_bwd, count),
        [struct(clips.shape, BF16)] * 2,
        [pad],
        *arrived,
        clips,
        cotangent,
        spatial_kernel,
    )
    if staged:
        grad_expand = scatter_grad(*shares, count, scale_factor, outs[0])
    else:
        whole = lax.dot_general(
            parts[0], scaled, (((0,), (0,)), ((), ())), preferred_element_type=F32
        )
        whole = lax.psum_scatter(whole, ("tm", "dp"), scatter_dimension=0, tiled=True)
        grad_expand = whole * scale_factor
    return (block_out, grad_clips, grad_expand)


def solution(mesh):
    in_specs = (
        P(("groups", "dp"), "tm", None, None, None),
        P(("groups", "dp"), "tm", None, None, None),
        P(),
        P(),
        P(),
        P(),
        P(),
    )
    out_specs = (
        P(("groups", "dp"), "tm", None, None, None),
        P(("groups", "dp"), "tm", None, None, None),
        P(("groups", "tm", "dp"), None),
    )
    return jax.shard_map(local, mesh=mesh, in_specs=in_specs, out_specs=out_specs, check_vma=False)
```
